32 devices in a mesh: groups: 2 (over x), ctx: 16 (over z, y, core).
Axes of the slice: x: 2, y: 2, z: 4, core: 2. Of those that a mesh axis runs over, the one named last changes fastest.
Arguments:
- queries: bfloat16 [4096, 36864], P(('groups', 'ctx')), parts along dimension 0, may hold values from -6 to 40
- prefix_latent: bfloat16 [32, 36864], P(('groups', 'ctx')), parts along dimension 0, may hold values from -6 to 6
- window_latent: bfloat16 [64, 36864], P(('groups', 'ctx')), parts along dimension 0, may hold values from -6 to 120
- index_queries: bfloat16 [4096, 8192], P(('groups', 'ctx')), parts along dimension 0, may hold values from -6 to 6
- index_weights: float32 [4096, 64], P(('groups', 'ctx')), parts along dimension 0, may hold values from -0.75 to 0.75
- prefix_index_keys: bfloat16 [2048, 128], P(('groups', 'ctx')), parts along dimension 0, may hold values from -6 to 6
- window_index_keys: bfloat16 [4096, 128], P(('groups', 'ctx')), parts along dimension 0, may hold values from -6 to 6
- picks: int32 [64, 12], P(('groups', 'ctx')), parts along dimension 0, may hold values from 0 to 47, as said below
Outputs:
- attention: bfloat16 [4096, 32768], P(('groups', 'ctx')), parts along dimension 0
- prefix_index: float32 [4096, 1024], P(('groups', 'ctx')), parts along dimension 0
- window_index: float32 [4096, 2048], P(('groups', 'ctx')), parts along dimension 0
The draws below stay inside these ranges and needn't reach their ends.
There are 2 independent parts, one for each index of `groups`. The reference program is written for one: setup_inputs(seed, part) draws one part's arguments, and reference() takes and returns one part's arrays. A program takes and returns all parts, laid end to end along the dimension named above; each array names one. Nothing has to cross between parts.
Inputs may be any that keep to these rules, and one draw needn't show every extreme that they name: `picks`: each row names 12 distinct key blocks, never one after its own query block, and always its own. The query blocks that lie on one index of ctx name together at most one key block held by any other index of ctx (a prefix block and window blocks lie where their rows are placed).
All inputs are finite; a program needn't handle non-finite values.
Results may differ from the reference program's by a relative error of at most 0.008.
Values may be sent and summed in bfloat16 or wider, within the bound.
No kernel may reach another device: no remote copies, remote signals or barrier semaphores. Data moves between devices by JAX's collectives and lax.ppermute only.
A program may use at most 192 MiB of HBM per device.

```python
import jax
import jax.numpy as jnp
from jax import lax

H = 64
LAT = 512
ROPE = 64
IH = 64
IDX = 128
BLK = 64
PICKS = 12
ROW = 576
TOKENS = 2048
PREFIX = 1024


def draw_queries(key, part):
    key = jax.random.fold_in(key, 11)
    row_width = LAT + ROPE
    base = jnp.clip(jax.random.normal(key, (TOKENS, H, row_width), jnp.float32), -6.0, 6.0)
    return base.reshape(TOKENS, H * row_width).astype(jnp.bfloat16)


def draw_window_latent(key, part):
    key = jax.random.fold_in(key, 23)
    row_width = LAT + ROPE
    query_blocks = TOKENS // BLK
    base = jnp.clip(jax.random.normal(key, (query_blocks, BLK, row_width), jnp.float32), -6.0, 6.0)
    return base.reshape(query_blocks, BLK * row_width).astype(jnp.bfloat16)


def draw_picks(key, part):
    key = jax.random.fold_in(key, 37)
    devices = PREFIX // BLK
    query_blocks = TOKENS // BLK
    per_device = query_blocks // devices
    total = devices + query_blocks
    key_index = jnp.arange(total, dtype=jnp.int32)
    owner = jnp.where(key_index < devices, key_index, (key_index - devices) // per_device)
    device_index = jnp.arange(devices, dtype=jnp.int32)
    open_device = jnp.logical_or(key_index[None, :] < devices, owner[None, :] < device_index[:, None])
    first_key, second_key = jax.random.split(key)
    spread = 2 ** 20
    ranked = jax.random.randint(first_key, (devices, total), 0, spread, jnp.int32) * total + key_index[None, :]
    ranked = jnp.where(open_device, ranked, -1)
    same_owner = owner[None, :] == owner[:, None]
    best = jnp.max(jnp.where(same_owner[None, :, :], ranked[:, None, :], -1), axis=2)
    in_pool = jnp.logical_and(open_device, ranked == best)
    forced_key = devices + device_index * per_device - 1
    forced_owner = owner[None, :] == device_index[:, None] - 1
    in_pool = jnp.where(forced_owner, key_index[None, :] == forced_key[:, None], in_pool)
    query_index = jnp.arange(query_blocks, dtype=jnp.int32)
    query_device = query_index // per_device
    own_key = devices + query_index
    visible = jnp.logical_or(key_index[None, :] < devices, key_index[None, :] <= own_key[:, None])
    local_key = owner[None, :] == query_device[:, None]
    usable = jnp.logical_and(visible, jnp.logical_or(local_key, in_pool[query_device]))
    large = spread * total
    noise = jax.random.randint(second_key, (query_blocks, total), 0, spread, jnp.int32) * total + key_index[None, :]
    priority = jnp.where(usable, noise, -1 - key_index[None, :])
    forced_here = jnp.logical_and(jnp.logical_and((query_index % per_device == 0)[:, None], key_index[None, :] == forced_key[query_device][:, None]), (query_device >= 1)[:, None])
    priority = jnp.where(forced_here, 2 * large, priority)
    priority = jnp.where(key_index[None, :] == own_key[:, None], 3 * large, priority)
    unused, chosen = lax.top_k(priority, PICKS)
    return chosen.astype(jnp.int32)


def steps_of(rng, extent, pieces, low, top_value):
    def one(position, shards_of):
        draws = jax.random.uniform(jax.random.fold_in(jax.random.fold_in(rng, 6), position), (shards_of,), jnp.float32, low / len(pieces), top_value / len(pieces))
        return jnp.repeat(jnp.exp(draws), extent[position] // shards_of).reshape((-1,) + (1,) * (len(extent) - position - 1))

    loudness = one(*pieces[0])
    for cut in pieces[1:]:
        loudness = loudness * one(*cut)
    return loudness


def gaussian(key, dims, deviation, limit, shards=(), kind=jnp.bfloat16):
    values = jax.random.normal(key, dims, jnp.float32) * deviation
    if len(shards) > 0:
        values = steps_of(key, dims, shards, -0.22, 0.18) * values
    return jnp.clip(values, min=-limit, max=limit).astype(kind)


def setup_inputs(seed: int = 0, part: int = 0) -> dict:
    arg_keys = jax.random.split(jax.random.key(seed), 9)
    part_keys = jax.random.split(jax.random.fold_in(arg_keys[8], part), 9)
    queries = draw_queries(jax.random.fold_in(jax.random.fold_in(arg_keys[8], part), 71), part)
    prefix_latent = gaussian(part_keys[1], (PREFIX // BLK, BLK * ROW), 1.0, 6.0, ((0, 16),))
    window_latent = draw_window_latent(jax.random.fold_in(jax.random.fold_in(arg_keys[8], part), 71), part)
    index_queries = gaussian(part_keys[3], (TOKENS, IH * IDX), 1.0, 6.0, ((0, 16),))
    index_weights = gaussian(part_keys[4], (TOKENS, IH), (IH ** -0.5), 0.75, ((0, 16),), jnp.float32)
    prefix_index_keys = gaussian(part_keys[5], (PREFIX, IDX), 1.0, 6.0, ((0, 16),))
    window_index_keys = gaussian(part_keys[6], (TOKENS, IDX), 1.0, 6.0, ((0, 16),))
    picks = draw_picks(jax.random.fold_in(jax.random.fold_in(arg_keys[8], part), 71), part)
    return dict(queries=queries, prefix_latent=prefix_latent, window_latent=window_latent, index_queries=index_queries, index_weights=index_weights, prefix_index_keys=prefix_index_keys, window_index_keys=window_index_keys, picks=picks)


score_scale = 192.0 ** -0.5
masked_low = -1.0e30


def reference(queries, prefix_latent, window_latent, index_queries, index_weights, prefix_index_keys, window_index_keys, picks):
    row_width = LAT + ROPE
    query_blocks = TOKENS // BLK
    prefix_blocks = PREFIX // BLK
    table = jnp.concatenate([prefix_latent, window_latent], 0).reshape(prefix_blocks + query_blocks, BLK, row_width)
    keys_all = jnp.concatenate([prefix_index_keys, window_index_keys], 0).astype(jnp.float32)
    key_place = jnp.concatenate([jnp.full((PREFIX,), -1, jnp.int32), jnp.arange(TOKENS, dtype=jnp.int32)])
    query_rows = queries.reshape(query_blocks, BLK, H, row_width)
    index_rows = index_queries.reshape(query_blocks, BLK, IH, IDX)
    weight_rows = index_weights.reshape(query_blocks, BLK, IH)
    inner = jnp.arange(BLK, dtype=jnp.int32)

    def one_block(block):
        chosen = picks[block]
        kv_rows = jnp.take(table, chosen, axis=0).reshape(PICKS * BLK, row_width)
        scores = jnp.einsum("qhd,kd->qhk", query_rows[block].astype(jnp.float32), kv_rows.astype(jnp.float32)) * score_scale
        own_mask = chosen == prefix_blocks + block
        allowed = jnp.logical_or(jnp.logical_not(own_mask)[None, :, None], inner[None, None, :] <= inner[:, None, None])
        allowed = allowed.reshape(BLK, 1, PICKS * BLK)
        scores = jnp.where(allowed, scores, masked_low)
        peak = jnp.max(scores, axis=-1, keepdims=True)
        weights = jnp.exp(scores - peak)
        total = jnp.sum(weights, axis=-1, keepdims=True)
        probs = (weights / total).astype(jnp.bfloat16)
        result = jnp.einsum("qhk,kd->qhd", probs.astype(jnp.float32), kv_rows[:, :LAT].astype(jnp.float32)).astype(jnp.bfloat16)
        inner_products = jnp.einsum("qjd,kd->qjk", index_rows[block].astype(jnp.float32), keys_all) * IDX ** -0.5
        value = jnp.sum(jax.nn.relu(inner_products) * weight_rows[block][:, :, None], axis=1)
        query_place = block * BLK + inner
        visible = key_place[None, :] <= query_place[:, None]
        value = jnp.where(visible, value, 0.0)
        return result, value

    results, values = lax.map(one_block, jnp.arange(query_blocks, dtype=jnp.int32))
    attention = results.reshape(TOKENS, H * LAT)
    values = values.reshape(TOKENS, PREFIX + TOKENS)
    return attention, values[:, :PREFIX], values[:, PREFIX:]
```

```python
import functools

import jax
import jax.numpy as jnp
from jax import lax
from jax.experimental import pallas as pl
from jax.experimental.pallas import tpu as pltpu
from jax.sharding import PartitionSpec as P

H = 64
LAT = 512
ROPE = 64
ROW = LAT + ROPE
WIDE = 640
IH = 64
IDX = 128
BLK = 64
LANES = 128
TILE = 256
TOK_TILE = 32
HEAD_STEP = 16
PAIRS = 8
GROUP = 8
LOW = -1.0e30
EXP2_SCALE = 192.0**-0.5 * 1.4426950408889634
VMEM = 48 * 2**20


def index_tile(iq_ref, wide_ref, keys):
    keys_t = keys.T
    rows = iq_ref.shape[0]
    parts = []
    for t0 in range(0, rows, TOK_TILE):
        acc = jnp.zeros((TOK_TILE, TILE), jnp.float32)
        for j0 in range(0, IH, HEAD_STEP):
            lhs = jnp.concatenate(
                [
                    iq_ref[t0 : t0 + TOK_TILE, j * IDX : (j + 1) * IDX]
                    for j in range(j0, j0 + HEAD_STEP)
                ],
                0,
            )
            prod = jnp.dot(lhs, keys_t, preferred_element_type=jnp.float32)
            for j in range(HEAD_STEP):
                weight = wide_ref[j0 + j, t0 : t0 + TOK_TILE, :]
                weight = jnp.concatenate([weight] * (TILE // LANES), 1)
                acc = acc + jnp.maximum(prod[j * TOK_TILE : (j + 1) * TOK_TILE], 0.0) * weight
        parts.append(acc)
    return jnp.concatenate(parts, 0)


def spread_weights(w_ref, wide_ref):
    for j in range(IH):
        wide_ref[j] = jnp.broadcast_to(w_ref[:, j : j + 1] * IDX**-0.5, wide_ref.shape[1:])


def index_near_kernel(rels, own_ref, iq_ref, w_ref, keys_ref, out_ref, wide_ref):
    own = own_ref[0]
    tok = iq_ref.shape[0]
    span = BLK + tok
    spread_weights(w_ref, wide_ref)

    @pl.loop(0, len(rels) // 2)
    def _(pair):
        first = keys_ref[pl.ds(pl.multiple_of(2 * pair * span + BLK, BLK), tok), :]
        second = keys_ref[pl.ds(pl.multiple_of((2 * pair + 1) * span + BLK, BLK), tok), :]
        value = index_tile(iq_ref, wide_ref, jnp.concatenate([first, second], 0))
        out_ref[2 * pair] = value[:, :LANES]
        out_ref[2 * pair + 1] = value[:, LANES:]


def index_far_kernel(
    near, far, own_ref, iq_ref, w_ref, near_ref, far_ref, done_ref, prefix_ref, window_ref,
    wide_ref, keys_ref, res_ref,
):
    own = own_ref[0]
    tok = iq_ref.shape[0]
    span = BLK + tok
    devices = len(near) + len(far)
    spread_weights(w_ref, wide_ref)
    for ref, rels in ((near_ref, near), (far_ref, far)):
        for n, rel in enumerate(rels):
            at = pl.multiple_of((own ^ rel) * BLK, BLK)
            keys_ref[pl.ds(at, BLK), :] = ref[n * span : n * span + BLK, :]
    base = devices * BLK
    for n in range(len(far)):
        keys_ref[base + n * tok : base + (n + 1) * tok, :] = far_ref[
            n * span + BLK : (n + 1) * span, :
        ]

    @pl.loop(0, keys_ref.shape[0] // TILE)
    def _(tile):
        keys = keys_ref[pl.ds(pl.multiple_of(tile * TILE, TILE), TILE), :]
        value = index_tile(iq_ref, wide_ref, keys)
        res_ref[2 * tile] = value[:, :LANES]
        res_ref[2 * tile + 1] = value[:, LANES:]

    for n in range(base // LANES):
        prefix_ref[:, n * LANES : (n + 1) * LANES] = res_ref[n]
    row = lax.broadcasted_iota(jnp.int32, (tok, LANES), 0)
    lane = lax.broadcasted_iota(jnp.int32, (tok, LANES), 1)
    for rels, ref, start in ((near, done_ref, 0), (far, res_ref, base // LANES)):
        for n, rel in enumerate(rels):
            other = own ^ rel
            seen = other * tok + lane <= own * tok + row
            window_ref[:, pl.ds(pl.multiple_of(other * tok, LANES), LANES)] = jnp.where(
                seen, ref[start + n], 0.0
            )


def attention_kernel(devices, own_ref, pick_ref, q_ref, *refs):
    shards = refs[:devices]
    out_ref, cache, raw, even_t, odd_t, need, sem = refs[devices:]
    block = pl.program_id(0)
    own = own_ref[0]
    picks = pick_ref.shape[1]

    def split(pick):
        window = pick - devices
        holder = jnp.where(window < 0, pick, window // 2)
        return holder ^ own, jnp.where(window < 0, 0, 1 + window % 2)

    def fetch(rel, inner, slot):
        return pltpu.make_async_copy(
            shards[rel].at[pl.ds(pl.multiple_of(inner * BLK, BLK), BLK)],
            cache.at[slot],
            sem.at[slot],
        )

    @pl.when((block == 0) & (pl.program_id(1) == 0))
    def _():
        for rel in range(devices):
            need[rel] = 0
        for b in range(pick_ref.shape[0]):
            for s in range(picks):
                rel, inner = split(pick_ref[b, s])
                need[rel] = inner
        for n in range(3):
            fetch(0, n, 0 if n == 0 else devices - 1 + n).start()
        for rel in range(1, devices):
            fetch(rel, need[rel], rel).start()
        for n in range(3):
            fetch(0, n, 0 if n == 0 else devices - 1 + n).wait()
        for rel in range(1, devices):
            fetch(rel, need[rel], rel).wait()

    @pl.when(pl.program_id(1) == 0)
    def _():
        own_pick = devices + own * 2 + block
        own_slot = jnp.int32(0)
        for s in range(picks):
            own_slot = jnp.where(pick_ref[block, s] == own_pick, s, own_slot)
        for s in range(picks):
            place = jnp.where(own_slot == s, picks - 1, own_slot if s == picks - 1 else s)
            rel, inner = split(pick_ref[block, s])
            slot = jnp.where((rel == 0) & (inner > 0), devices - 1 + inner, rel)
            raw[pl.ds(pl.multiple_of(place * BLK, BLK), BLK), :] = cache[slot]
        turned = raw[...].T
        even_t[...] = turned
        odd_t[0:ROPE] = turned[ROW:WIDE]
        odd_t[ROPE:WIDE] = turned[0:ROW]

    count = picks * BLK
    row = lax.broadcasted_iota(jnp.int32, (BLK, LANES), 0)
    lane = lax.broadcasted_iota(jnp.int32, (BLK, LANES), 1)
    allowed = jnp.concatenate([lane - BLK <= row] * GROUP, 0)

    def score(unit):
        odd, first = unit % 2, unit // 2 * GROUP
        lhs = jnp.concatenate(
            [
                q_ref[:, (first + g) * 2 * ROW + odd * LAT : (first + g) * 2 * ROW + odd * LAT + WIDE]
                for g in range(GROUP)
            ],
            0,
        )
        return jnp.dot(lhs, (odd_t if odd else even_t)[...], preferred_element_type=jnp.float32)

    def finish(unit, scores):
        odd, first = unit % 2, unit // 2 * GROUP
        last = jnp.where(allowed, scores[:, count - LANES :], LOW)
        scores = jnp.concatenate([scores[:, : count - LANES], last], 1)
        peak = jnp.max(scores, axis=1, keepdims=True)
        weights = jnp.exp2((scores - peak) * EXP2_SCALE)
        total = jnp.sum(weights, axis=1, keepdims=True)
        result = jnp.dot(
            weights.astype(jnp.bfloat16), raw[:, :LAT], preferred_element_type=jnp.float32
        )
        result = (result * (1.0 / total)).astype(jnp.bfloat16)
        for g in range(GROUP):
            at = (first + g) * 2 * LAT + odd * LAT
            out_ref[:, at : at + LAT] = result[g * BLK : (g + 1) * BLK]

    units = PAIRS // GROUP * 2
    scores = score(0)
    for unit in range(units):
        following = score(unit + 1) if unit + 1 < units else None
        finish(unit, scores)
        scores = following


def body(
    queries,
    prefix_latent,
    window_latent,
    index_queries,
    index_weights,
    prefix_index_keys,
    window_index_keys,
    picks,
):
    devices = lax.axis_size("ctx")
    own = lax.axis_index("ctx").astype(jnp.int32).reshape(1)
    tok = queries.shape[0]
    per_device = tok // BLK
    span = BLK + tok

    def swap(array, rel):
        return lax.ppermute(array, "ctx", [(i, i ^ rel) for i in range(devices)])

    line = list(range(0, devices, 4))
    keys = jnp.concatenate([prefix_index_keys, window_index_keys], 0)
    key_line = jnp.concatenate([keys] + [swap(keys, rel) for rel in line[1:]], 0)
    near_keys = jnp.concatenate([key_line, swap(key_line, 2)], 0)
    near = line + [rel + 2 for rel in line]
    far_keys = swap(near_keys, 1)
    far = [rel + 1 for rel in near]

    rows = jnp.concatenate([prefix_latent, window_latent], 0).reshape(3 * BLK, ROW)
    rows = jnp.pad(rows, ((0, 0), (0, WIDE - ROW)))
    shards = [None] * devices
    shards[0] = rows
    for rel in line[1:]:
        shards[rel] = swap(rows, rel)
    for rel in line:
        shards[rel + 2] = swap(shards[rel], 2)
    for rel in near:
        shards[rel + 1] = swap(shards[rel], 1)

    smem = pl.BlockSpec(memory_space=pltpu.SMEM)
    vmem = pl.BlockSpec(memory_space=pltpu.VMEM)
    hbm = pl.BlockSpec(memory_space=pl.ANY)
    params = pltpu.CompilerParams(vmem_limit_bytes=VMEM)
    done = pl.pallas_call(
        functools.partial(index_near_kernel, near),
        out_shape=jax.ShapeDtypeStruct((len(near), tok, LANES), jnp.float32),
        in_specs=[smem, vmem, vmem, vmem],
        out_specs=vmem,
        scratch_shapes=[pltpu.VMEM((IH, tok, LANES), jnp.float32)],
        compiler_params=params,
        cost_estimate=pl.CostEstimate(
            flops=2 * tok * IH * IDX * len(near) * tok * 4, bytes_accessed=2**22, transcendentals=0
        ),
    )(own, index_queries, index_weights, near_keys)
    total_keys = devices * BLK + len(far) * tok
    prefix_index, window_index = pl.pallas_call(
        functools.partial(index_far_kernel, near, far),
        out_shape=(
            jax.ShapeDtypeStruct((tok, devices * BLK), jnp.float32),
            jax.ShapeDtypeStruct((tok, devices * tok), jnp.float32),
        ),
        in_specs=[smem, vmem, vmem, vmem, vmem, vmem],
        out_specs=(vmem, vmem),
        scratch_shapes=[
            pltpu.VMEM((IH, tok, LANES), jnp.float32),
            pltpu.VMEM((total_keys, IDX), jnp.bfloat16),
            pltpu.VMEM((total_keys // LANES, tok, LANES), jnp.float32),
        ],
        compiler_params=params,
        cost_estimate=pl.CostEstimate(
            flops=2 * tok * IH * IDX * total_keys * 4, bytes_accessed=2**22, transcendentals=0
        ),
    )(own, index_queries, index_weights, near_keys, far_keys, done)

    count = picks.shape[1] * BLK
    attention = pl.pallas_call(
        functools.partial(attention_kernel, devices),
        grid_spec=pltpu.PrefetchScalarGridSpec(
            num_scalar_prefetch=2,
            grid=(per_device, H // 2 // PAIRS),
            in_specs=[pl.BlockSpec((BLK, PAIRS * 2 * ROW), lambda b, h, *_: (b, h))]
            + [hbm] * devices,
            out_specs=pl.BlockSpec((BLK, PAIRS * 2 * LAT), lambda b, h, *_: (b, h)),
            scratch_shapes=[
                pltpu.VMEM((devices + 2, BLK, WIDE), jnp.bfloat16),
                pltpu.VMEM((count, WIDE), jnp.bfloat16),
                pltpu.VMEM((WIDE, count), jnp.bfloat16),
                pltpu.VMEM((WIDE, count), jnp.bfloat16),
                pltpu.SMEM((devices,), jnp.int32),
                pltpu.SemaphoreType.DMA((devices + 2,)),
            ],
        ),
        out_shape=jax.ShapeDtypeStruct((tok, H * LAT), jnp.bfloat16),
        compiler_params=params,
        cost_estimate=pl.CostEstimate(
            flops=2 * tok * H * count * (WIDE + LAT), bytes_accessed=2**24, transcendentals=0
        ),
    )(own, picks, queries, *shards)
    return (attention, prefix_index, window_index)


def solution(mesh):
    placed = P(("groups", "ctx"), None)
    return jax.shard_map(
        body,
        mesh=mesh,
        in_specs=(placed,) * 8,
        out_specs=(placed,) * 3,
        check_vma=False,
    )
```

```python
import functools

import jax
import jax.numpy as jnp
from jax import lax
from jax.experimental import pallas as pl
from jax.experimental.pallas import tpu as pltpu
from jax.sharding import PartitionSpec as P

H = 64
LAT = 512
ROPE = 64
ROW = LAT + ROPE
WIDE = 640
IH = 64
IDX = 128
BLK = 64
LANES = 128
TILE = 256
TOK_TILE = 32
HEAD_STEP = 16
PAIRS = 8
GROUP = 8
LOW = -1.0e30
EXP2_SCALE = 192.0**-0.5 * 1.4426950408889634
VMEM = 48 * 2**20


def index_tile(iq_ref, wide_ref, keys):
    keys_t = keys.T
    rows = iq_ref.shape[0]
    parts = []
    for t0 in range(0, rows, TOK_TILE):
        acc = jnp.zeros((TOK_TILE, TILE), jnp.float32)
        for j0 in range(0, IH, HEAD_STEP):
            lhs = jnp.concatenate(
                [
                    iq_ref[t0 : t0 + TOK_TILE, j * IDX : (j + 1) * IDX]
                    for j in range(j0, j0 + HEAD_STEP)
                ],
                0,
            )
            prod = jnp.dot(lhs, keys_t, preferred_element_type=jnp.float32)
            for j in range(HEAD_STEP):
                weight = wide_ref[j0 + j, t0 : t0 + TOK_TILE, :]
                weight = jnp.concatenate([weight] * (TILE // LANES), 1)
                acc = acc + jnp.maximum(prod[j * TOK_TILE : (j + 1) * TOK_TILE], 0.0) * weight
        parts.append(acc)
    return jnp.concatenate(parts, 0)


def spread_weights(w_ref, wide_ref):
    for j in range(IH):
        wide_ref[j] = jnp.broadcast_to(w_ref[:, j : j + 1] * IDX**-0.5, wide_ref.shape[1:])


def index_window_kernel(rels, iq_ref, w_ref, keys_ref, out_ref, wide_ref):
    tok = iq_ref.shape[0]
    span = BLK + tok
    spread_weights(w_ref, wide_ref)

    @pl.loop(0, len(rels) // 2)
    def _(pair):
        first = keys_ref[pl.ds(pl.multiple_of(2 * pair * span + BLK, BLK), tok), :]
        second = keys_ref[pl.ds(pl.multiple_of((2 * pair + 1) * span + BLK, BLK), tok), :]
        value = index_tile(iq_ref, wide_ref, jnp.concatenate([first, second], 0))
        out_ref[2 * pair] = value[:, :LANES]
        out_ref[2 * pair + 1] = value[:, LANES:]


def index_prefix_kernel(
    near, far, own_ref, iq_ref, w_ref, near_ref, far_ref, near_done, far_done, prefix_ref,
    window_ref, wide_ref, keys_ref, res_ref,
):
    own = own_ref[0]
    tok = iq_ref.shape[0]
    span = BLK + tok
    spread_weights(w_ref, wide_ref)
    for ref, rels in ((near_ref, near), (far_ref, far)):
        for n, rel in enumerate(rels):
            at = pl.multiple_of((own ^ rel) * BLK, BLK)
            keys_ref[pl.ds(at, BLK), :] = ref[n * span : n * span + BLK, :]

    @pl.loop(0, keys_ref.shape[0] // TILE)
    def _(tile):
        keys = keys_ref[pl.ds(pl.multiple_of(tile * TILE, TILE), TILE), :]
        value = index_tile(iq_ref, wide_ref, keys)
        res_ref[2 * tile] = value[:, :LANES]
        res_ref[2 * tile + 1] = value[:, LANES:]

    for n in range(keys_ref.shape[0] // LANES):
        prefix_ref[:, n * LANES : (n + 1) * LANES] = res_ref[n]
    row = lax.broadcasted_iota(jnp.int32, (tok, LANES), 0)
    lane = lax.broadcasted_iota(jnp.int32, (tok, LANES), 1)
    for rels, ref in ((near, near_done), (far, far_done)):
        for n, rel in enumerate(rels):
            other = own ^ rel
            seen = other * tok + lane <= own * tok + row
            window_ref[:, pl.ds(pl.multiple_of(other * tok, LANES), LANES)] = jnp.where(
                seen, ref[n], 0.0
            )


def attention_kernel(devices, own_ref, pick_ref, q_ref, *refs):
    shards = refs[:devices]
    out_ref, cache, raw, even_t, odd_t, need, sem = refs[devices:]
    block = pl.program_id(0)
    own = own_ref[0]
    picks = pick_ref.shape[1]

    def split(pick):
        window = pick - devices
        holder = jnp.where(window < 0, pick, window // 2)
        return holder ^ own, jnp.where(window < 0, 0, 1 + window % 2)

    def fetch(rel, inner, slot):
        return pltpu.make_async_copy(
            shards[rel].at[pl.ds(pl.multiple_of(inner * BLK, BLK), BLK)],
            cache.at[slot],
            sem.at[slot],
        )

    @pl.when((block == 0) & (pl.program_id(1) == 0))
    def _():
        for rel in range(devices):
            need[rel] = 0
        for b in range(pick_ref.shape[0]):
            for s in range(picks):
                rel, inner = split(pick_ref[b, s])
                need[rel] = inner
        for n in range(3):
            fetch(0, n, 0 if n == 0 else devices - 1 + n).start()
        for rel in range(1, devices):
            fetch(rel, need[rel], rel).start()
        for n in range(3):
            fetch(0, n, 0 if n == 0 else devices - 1 + n).wait()
        for rel in range(1, devices):
            fetch(rel, need[rel], rel).wait()

    @pl.when(pl.program_id(1) == 0)
    def _():
        own_pick = devices + own * 2 + block
        own_slot = jnp.int32(0)
        for s in range(picks):
            own_slot = jnp.where(pick_ref[block, s] == own_pick, s, own_slot)
        for s in range(picks):
            place = jnp.where(own_slot == s, picks - 1, own_slot if s == picks - 1 else s)
            rel, inner = split(pick_ref[block, s])
            slot = jnp.where((rel == 0) & (inner > 0), devices - 1 + inner, rel)
            raw[pl.ds(pl.multiple_of(place * BLK, BLK), BLK), :] = cache[slot]
        turned = raw[...].T
        even_t[...] = turned
        odd_t[0:ROPE] = turned[ROW:WIDE]
        odd_t[ROPE:WIDE] = turned[0:ROW]

    count = picks * BLK
    row = lax.broadcasted_iota(jnp.int32, (BLK, LANES), 0)
    lane = lax.broadcasted_iota(jnp.int32, (BLK, LANES), 1)
    allowed = jnp.concatenate([lane - BLK <= row] * GROUP, 0)

    def score(unit):
        odd, first = unit % 2, unit // 2 * GROUP
        lhs = jnp.concatenate(
            [
                q_ref[:, (first + g) * 2 * ROW + odd * LAT : (first + g) * 2 * ROW + odd * LAT + WIDE]
                for g in range(GROUP)
            ],
            0,
        )
        return jnp.dot(lhs, (odd_t if odd else even_t)[...], preferred_element_type=jnp.float32)

    def finish(unit, scores):
        odd, first = unit % 2, unit // 2 * GROUP
        last = jnp.where(allowed, scores[:, count - LANES :], LOW)
        scores = jnp.concatenate([scores[:, : count - LANES], last], 1)
        peak = jnp.max(scores, axis=1, keepdims=True)
        weights = jnp.exp2((scores - peak) * EXP2_SCALE)
        total = jnp.sum(weights, axis=1, keepdims=True)
        result = jnp.dot(
            weights.astype(jnp.bfloat16), raw[:, :LAT], preferred_element_type=jnp.float32
        )
        result = (result * (1.0 / total)).astype(jnp.bfloat16)
        for g in range(GROUP):
            at = (first + g) * 2 * LAT + odd * LAT
            out_ref[:, at : at + LAT] = result[g * BLK : (g + 1) * BLK]

    units = PAIRS // GROUP * 2
    scores = score(0)
    for unit in range(units):
        following = score(unit + 1) if unit + 1 < units else None
        finish(unit, scores)
        scores = following


def body(
    queries,
    prefix_latent,
    window_latent,
    index_queries,
    index_weights,
    prefix_index_keys,
    window_index_keys,
    picks,
):
    devices = lax.axis_size("ctx")
    own = lax.axis_index("ctx").astype(jnp.int32).reshape(1)
    tok = queries.shape[0]
    per_device = tok // BLK
    span = BLK + tok

    def swap(array, rel):
        return lax.ppermute(array, "ctx", [(i, i ^ rel) for i in range(devices)])

    smem = pl.BlockSpec(memory_space=pltpu.SMEM)
    vmem = pl.BlockSpec(memory_space=pltpu.VMEM)
    hbm = pl.BlockSpec(memory_space=pl.ANY)
    params = pltpu.CompilerParams(vmem_limit_bytes=VMEM)

    def index_cost(keys):
        return pl.CostEstimate(
            flops=2 * tok * IH * IDX * keys * 4, bytes_accessed=2**22, transcendentals=0
        )

    def index_window(rels, shard_keys):
        return pl.pallas_call(
            functools.partial(index_window_kernel, rels),
            out_shape=jax.ShapeDtypeStruct((len(rels), tok, LANES), jnp.float32),
            in_specs=[vmem, vmem, vmem],
            out_specs=vmem,
            scratch_shapes=[pltpu.VMEM((IH, tok, LANES), jnp.float32)],
            compiler_params=params,
            cost_estimate=index_cost(len(rels) * tok),
        )(index_queries, index_weights, shard_keys)

    def after(done, *arrays):
        return lax.optimization_barrier((done, *arrays))[1:]

    line = list(range(0, devices, 4))
    keys = jnp.concatenate([prefix_index_keys, window_index_keys], 0)
    key_line = jnp.concatenate([keys] + [swap(keys, rel) for rel in line[1:]], 0)
    near_keys = jnp.concatenate([key_line, swap(key_line, 2)], 0)
    near = line + [rel + 2 for rel in line]
    far_keys = swap(near_keys, 1)
    far = [rel + 1 for rel in near]

    rows = jnp.concatenate([prefix_latent, window_latent], 0).reshape(3 * BLK, ROW)
    rows = jnp.pad(rows, ((0, 0), (0, WIDE - ROW)))
    shards = [None] * devices
    shards[0] = rows
    for rel in line[1:]:
        shards[rel] = swap(rows, rel)
    shards[2] = swap(rows, 2)

    near_done = index_window(near, near_keys)
    first, rest = line[1], line[2:]
    held = [0, 2, first]
    for rel, array in zip(held, after(near_done, *[shards[rel] for rel in held])):
        shards[rel + 1] = swap(array, 1)
        if rel == first:
            shards[rel + 2] = swap(array, 2)
    far_done = index_window(far, far_keys)
    held = rest + [first + 2]
    for rel, array in zip(held, after(far_done, *[shards[rel] for rel in held])):
        shards[rel + 1] = swap(array, 1)
        if rel in rest:
            shards[rel + 2] = swap(array, 2)

    prefix_index, window_index = pl.pallas_call(
        functools.partial(index_prefix_kernel, near, far),
        out_shape=(
            jax.ShapeDtypeStruct((tok, devices * BLK), jnp.float32),
            jax.ShapeDtypeStruct((tok, devices * tok), jnp.float32),
        ),
        in_specs=[smem] + [vmem] * 6,
        out_specs=(vmem, vmem),
        scratch_shapes=[
            pltpu.VMEM((IH, tok, LANES), jnp.float32),
            pltpu.VMEM((devices * BLK, IDX), jnp.bfloat16),
            pltpu.VMEM((devices * BLK // LANES, tok, LANES), jnp.float32),
        ],
        compiler_params=params,
        cost_estimate=index_cost(devices * BLK),
    )(own, index_queries, index_weights, near_keys, far_keys, near_done, far_done)
    held = [rel + 2 for rel in rest]
    for rel, array in zip(held, after(prefix_index, *[shards[rel] for rel in held])):
        shards[rel + 1] = swap(array, 1)

    count = picks.shape[1] * BLK
    attention = pl.pallas_call(
        functools.partial(attention_kernel, devices),
        grid_spec=pltpu.PrefetchScalarGridSpec(
            num_scalar_prefetch=2,
            grid=(per_device, H // 2 // PAIRS),
            in_specs=[pl.BlockSpec((BLK, PAIRS * 2 * ROW), lambda b, h, *_: (b, h))]
            + [hbm] * devices,
            out_specs=pl.BlockSpec((BLK, PAIRS * 2 * LAT), lambda b, h, *_: (b, h)),
            scratch_shapes=[
                pltpu.VMEM((devices + 2, BLK, WIDE), jnp.bfloat16),
                pltpu.VMEM((count, WIDE), jnp.bfloat16),
                pltpu.VMEM((WIDE, count), jnp.bfloat16),
                pltpu.VMEM((WIDE, count), jnp.bfloat16),
                pltpu.SMEM((devices,), jnp.int32),
                pltpu.SemaphoreType.DMA((devices + 2,)),
            ],
        ),
        out_shape=jax.ShapeDtypeStruct((tok, H * LAT), jnp.bfloat16),
        compiler_params=params,
        cost_estimate=pl.CostEstimate(
            flops=2 * tok * H * count * (WIDE + LAT), bytes_accessed=2**24, transcendentals=0
        ),
    )(own, picks, queries, *shards)
    return (attention, prefix_index, window_index)


def solution(mesh):
    placed = P(("groups", "ctx"), None)
    return jax.shard_map(
        body,
        mesh=mesh,
        in_specs=(placed,) * 8,
        out_specs=(placed,) * 3,
        check_vma=False,
    )
```

```python
import functools

import jax
import jax.numpy as jnp
from jax import lax
from jax.experimental import pallas as pl
from jax.experimental.pallas import tpu as pltpu
from jax.sharding import PartitionSpec as P

H = 64
LAT = 512
ROPE = 64
ROW = LAT + ROPE
WIDE = 640
IH = 64
IDX = 128
BLK = 64
LANES = 128
TILE = 512
TOK_TILE = 32
HEAD_STEP = 16
PAIRS = 8
GROUP = 8
LOW = -1.0e30
EXP2_SCALE = 192.0**-0.5 * 1.4426950408889634
VMEM = 48 * 2**20


def index_tile(iq_ref, weights, keys):
    keys_t = keys.T
    rows, width = iq_ref.shape[0], keys.shape[0]
    parts = []
    for t0 in range(0, rows, TOK_TILE):
        acc = jnp.zeros((TOK_TILE, width), jnp.float32)
        for j0 in range(0, IH, HEAD_STEP):
            lhs = jnp.concatenate(
                [
                    iq_ref[t0 : t0 + TOK_TILE, j * IDX : (j + 1) * IDX]
                    for j in range(j0, j0 + HEAD_STEP)
                ],
                0,
            )
            prod = jnp.dot(lhs, keys_t, preferred_element_type=jnp.float32)
            for j in range(HEAD_STEP):
                weight = jnp.broadcast_to(
                    weights[t0 : t0 + TOK_TILE, j0 + j : j0 + j + 1], (TOK_TILE, LANES)
                )
                weight = jnp.concatenate([weight] * (width // LANES), 1)
                acc = acc + jnp.maximum(prod[j * TOK_TILE : (j + 1) * TOK_TILE], 0.0) * weight
        parts.append(acc)
    return jnp.concatenate(parts, 0)


def index_window_kernel(shards, iq_ref, w_ref, keys_ref, out_ref):
    tok = iq_ref.shape[0]
    span = BLK + tok
    each = TILE // tok
    weights = w_ref[...].T * IDX**-0.5

    @pl.loop(0, shards // each)
    def _(step):
        keys = [
            keys_ref[pl.ds(pl.multiple_of((step * each + n) * span + BLK, BLK), tok), :]
            for n in range(each)
        ]
        value = index_tile(iq_ref, weights, jnp.concatenate(keys, 0))
        for n in range(each):
            out_ref[step * each + n] = value[:, n * tok : (n + 1) * tok]


def index_prefix_kernel(places, *refs):
    count = len(places)
    own_ref, iq_ref, w_ref = refs[:3]
    key_refs, done_refs = refs[3 : 3 + count], refs[3 + count : 3 + 2 * count]
    prefix_ref, window_ref, keys_ref = refs[3 + 2 * count :]
    own = own_ref[0]
    tok = iq_ref.shape[0]
    span = BLK + tok
    weights = w_ref[...].T * IDX**-0.5
    for ref, rels in zip(key_refs, places):
        for n, rel in enumerate(rels):
            at = pl.multiple_of((own ^ rel) * BLK, BLK)
            keys_ref[pl.ds(at, BLK), :] = ref[n * span : n * span + BLK, :]
    row = lax.broadcasted_iota(jnp.int32, (tok, LANES), 0)
    lane = lax.broadcasted_iota(jnp.int32, (tok, LANES), 1)
    for ref, rels in zip(done_refs, places):
        for n, rel in enumerate(rels):
            other = own ^ rel
            seen = other * tok + lane <= own * tok + row
            window_ref[:, pl.ds(pl.multiple_of(other * tok, LANES), LANES)] = jnp.where(
                seen, ref[n], 0.0
            )

    @pl.loop(0, keys_ref.shape[0] // TILE)
    def _(step):
        at = pl.multiple_of(step * TILE, TILE)
        prefix_ref[:, pl.ds(at, TILE)] = index_tile(iq_ref, weights, keys_ref[pl.ds(at, TILE), :])


def attention_kernel(devices, own_ref, pick_ref, q_ref, *refs):
    shards = refs[:devices]
    out_ref, cache, raw, even_t, odd_t, need, sem = refs[devices:]
    block = pl.program_id(0)
    own = own_ref[0]
    picks = pick_ref.shape[1]

    def split(pick):
        window = pick - devices
        holder = jnp.where(window < 0, pick, window // 2)
        return holder ^ own, jnp.where(window < 0, 0, 1 + window % 2)

    def fetch(rel, inner, slot):
        return pltpu.make_async_copy(
            shards[rel].at[pl.ds(pl.multiple_of(inner * BLK, BLK), BLK)],
            cache.at[slot],
            sem.at[slot],
        )

    @pl.when((block == 0) & (pl.program_id(1) == 0))
    def _():
        for rel in range(devices):
            need[rel] = 0
        for b in range(pick_ref.shape[0]):
            for s in range(picks):
                rel, inner = split(pick_ref[b, s])
                need[rel] = inner
        for n in range(3):
            fetch(0, n, 0 if n == 0 else devices - 1 + n).start()
        for rel in range(1, devices):
            fetch(rel, need[rel], rel).start()
        for n in range(3):
            fetch(0, n, 0 if n == 0 else devices - 1 + n).wait()
        for rel in range(1, devices):
            fetch(rel, need[rel], rel).wait()

    @pl.when(pl.program_id(1) == 0)
    def _():
        own_pick = devices + own * 2 + block
        own_slot = jnp.int32(0)
        for s in range(picks):
            own_slot = jnp.where(pick_ref[block, s] == own_pick, s, own_slot)
        for s in range(picks):
            place = jnp.where(own_slot == s, picks - 1, own_slot if s == picks - 1 else s)
            rel, inner = split(pick_ref[block, s])
            slot = jnp.where((rel == 0) & (inner > 0), devices - 1 + inner, rel)
            raw[pl.ds(pl.multiple_of(place * BLK, BLK), BLK), :] = cache[slot]
        turned = raw[...].T
        even_t[...] = turned
        odd_t[0:ROPE] = turned[ROW:WIDE]
        odd_t[ROPE:WIDE] = turned[0:ROW]

    count = picks * BLK
    row = lax.broadcasted_iota(jnp.int32, (BLK, LANES), 0)
    lane = lax.broadcasted_iota(jnp.int32, (BLK, LANES), 1)
    allowed = jnp.concatenate([lane - BLK <= row] * GROUP, 0)

    def score(unit):
        odd, first = unit % 2, unit // 2 * GROUP
        lhs = jnp.concatenate(
            [
                q_ref[:, (first + g) * 2 * ROW + odd * LAT : (first + g) * 2 * ROW + odd * LAT + WIDE]
                for g in range(GROUP)
            ],
            0,
        )
        return jnp.dot(lhs, (odd_t if odd else even_t)[...], preferred_element_type=jnp.float32)

    def finish(unit, scores):
        odd, first = unit % 2, unit // 2 * GROUP
        last = jnp.where(allowed, scores[:, count - LANES :], LOW)
        scores = jnp.concatenate([scores[:, : count - LANES], last], 1)
        peak = jnp.max(scores, axis=1, keepdims=True)
        weights = jnp.exp2((scores - peak) * EXP2_SCALE)
        total = jnp.sum(weights, axis=1, keepdims=True)
        result = jnp.dot(
            weights.astype(jnp.bfloat16), raw[:, :LAT], preferred_element_type=jnp.float32
        )
        result = (result * (1.0 / total)).astype(jnp.bfloat16)
        for g in range(GROUP):
            at = (first + g) * 2 * LAT + odd * LAT
            out_ref[:, at : at + LAT] = result[g * BLK : (g + 1) * BLK]

    units = PAIRS // GROUP * 2
    scores = score(0)
    for unit in range(units):
        following = score(unit + 1) if unit + 1 < units else None
        finish(unit, scores)
        scores = following


def body(
    queries,
    prefix_latent,
    window_latent,
    index_queries,
    index_weights,
    prefix_index_keys,
    window_index_keys,
    picks,
):
    devices = lax.axis_size("ctx")
    own = lax.axis_index("ctx").astype(jnp.int32).reshape(1)
    tok = queries.shape[0]
    per_device = tok // BLK
    span = BLK + tok

    def swap(array, rel):
        return lax.ppermute(array, "ctx", [(i, i ^ rel) for i in range(devices)])

    smem = pl.BlockSpec(memory_space=pltpu.SMEM)
    vmem = pl.BlockSpec(memory_space=pltpu.VMEM)
    hbm = pl.BlockSpec(memory_space=pl.ANY)
    params = pltpu.CompilerParams(vmem_limit_bytes=VMEM)

    def index_cost(keys):
        return pl.CostEstimate(
            flops=2 * tok * IH * IDX * keys * 4, bytes_accessed=2**22, transcendentals=0
        )

    weights = index_weights.T

    def index_window(shard_keys):
        count = shard_keys.shape[0] // span
        return pl.pallas_call(
            functools.partial(index_window_kernel, count),
            out_shape=jax.ShapeDtypeStruct((count, tok, LANES), jnp.float32),
            in_specs=[vmem, vmem, vmem],
            out_specs=vmem,
            compiler_params=params,
            cost_estimate=index_cost(count * tok),
        )(index_queries, weights, shard_keys)

    def after(done, *arrays):
        return lax.optimization_barrier((done, *arrays))[1:]

    bits = []
    bit = devices // 2
    while bit >= 4:
        bits.append(bit)
        bit //= 2

    rows = jnp.concatenate([prefix_latent, window_latent], 0).reshape(3 * BLK, ROW)
    rows = jnp.pad(rows, ((0, 0), (0, WIDE - ROW)))
    shards = {0: rows}
    for bit in bits + [2]:
        shards[bit] = swap(rows, bit)

    line, key_line = [0], jnp.concatenate([prefix_index_keys, window_index_keys], 0)
    (key_line,) = after(rows, key_line)
    for bit in bits:
        key_line = jnp.concatenate([key_line, swap(key_line, bit)], 0)
        line = line + [rel ^ bit for rel in line]
    key_side = swap(key_line, 2)
    side = [rel ^ 2 for rel in line]
    key_far = swap(jnp.concatenate([key_line, key_side], 0), 1)
    far = [rel ^ 1 for rel in line + side]

    low, high = bits[-1], bits[:-1]

    def send(done, *moves):
        sources = sorted({rel for rel, _ in moves})
        held = dict(zip(sources, after(done, *[shards[rel] for rel in sources])))
        for rel, bit in moves:
            shards[rel ^ bit] = swap(held[rel], bit)

    line_done = index_window(key_line)
    send(line_done, (0, 1), (2, 1), (low, 2), (low, 1))
    side_done = index_window(key_side)
    reach = list(high)
    moves = []
    for n, bit in enumerate(high):
        moves += [(bit, 2), (bit, 1)]
    send(side_done, *moves)
    rest = []
    for n, bit in enumerate(high):
        for other in bits[n + 1 :]:
            for rel in [r for r in [bit] + rest if not r & (2 * other - 1) and r & -r > other]:
                (held,) = after(side_done, shards[rel])
                shards[rel ^ other] = swap(held, other)
                rest.append(rel ^ other)
    far_done = index_window(key_far)
    send(
        far_done,
        (low | 2, 1),
        *[(bit | 2, 1) for bit in high],
        *[(rel, 2) for rel in rest],
        *[(rel, 1) for rel in rest],
    )

    prefix_index, window_index = pl.pallas_call(
        functools.partial(index_prefix_kernel, [line, side, far]),
        out_shape=(
            jax.ShapeDtypeStruct((tok, devices * BLK), jnp.float32),
            jax.ShapeDtypeStruct((tok, devices * tok), jnp.float32),
        ),
        in_specs=[smem] + [vmem] * 8,
        out_specs=(vmem, vmem),
        scratch_shapes=[pltpu.VMEM((devices * BLK, IDX), jnp.bfloat16)],
        compiler_params=params,
        cost_estimate=index_cost(devices * BLK),
    )(
        own,
        index_queries,
        weights,
        key_line,
        key_side,
        key_far,
        line_done,
        side_done,
        far_done,
    )
    send(prefix_index, *[(rel | 2, 1) for rel in rest])
    shards = [shards[rel] for rel in range(devices)]

    count = picks.shape[1] * BLK
    attention = pl.pallas_call(
        functools.partial(attention_kernel, devices),
        grid_spec=pltpu.PrefetchScalarGridSpec(
            num_scalar_prefetch=2,
            grid=(per_device, H // 2 // PAIRS),
            in_specs=[pl.BlockSpec((BLK, PAIRS * 2 * ROW), lambda b, h, *_: (b, h))]
            + [hbm] * devices,
            out_specs=pl.BlockSpec((BLK, PAIRS * 2 * LAT), lambda b, h, *_: (b, h)),
            scratch_shapes=[
                pltpu.VMEM((devices + 2, BLK, WIDE), jnp.bfloat16),
                pltpu.VMEM((count, WIDE), jnp.bfloat16),
                pltpu.VMEM((WIDE, count), jnp.bfloat16),
                pltpu.VMEM((WIDE, count), jnp.bfloat16),
                pltpu.SMEM((devices,), jnp.int32),
                pltpu.SemaphoreType.DMA((devices + 2,)),
            ],
        ),
        out_shape=jax.ShapeDtypeStruct((tok, H * LAT), jnp.bfloat16),
        compiler_params=params,
        cost_estimate=pl.CostEstimate(
            flops=2 * tok * H * count * (WIDE + LAT), bytes_accessed=2**24, transcendentals=0
        ),
    )(own, picks, queries, *shards)
    return (attention, prefix_index, window_index)


def solution(mesh):
    placed = P(("groups", "ctx"), None)
    return jax.shard_map(
        body,
        mesh=mesh,
        in_specs=(placed,) * 8,
        out_specs=(placed,) * 3,
        check_vma=False,
    )
```

```python
import functools

import jax
import jax.numpy as jnp
from jax import lax
from jax.experimental import pallas as pl
from jax.experimental.pallas import tpu as pltpu
from jax.sharding import PartitionSpec as P

H = 64
LAT = 512
ROPE = 64
ROW = LAT + ROPE
WIDE = 640
IH = 64
IDX = 128
BLK = 64
LANES = 128
TILE = 512
TOK_TILE = 32
HEAD_STEP = 16
PAIRS = 8
GROUP = 8
LOW = -1.0e30
EXP2_SCALE = 192.0**-0.5 * 1.4426950408889634
VMEM = 48 * 2**20


def index_tile(iq_ref, weights, keys, pieces=None):
    keys_t = keys.T
    rows, width = iq_ref.shape[0], keys.shape[0]
    parts = []
    for t0 in range(0, rows, TOK_TILE):
        if pieces is not None:
            pieces[t0 // TOK_TILE].wait()
        acc = jnp.zeros((TOK_TILE, width), jnp.float32)
        for j0 in range(0, IH, HEAD_STEP):
            lhs = jnp.concatenate(
                [
                    iq_ref[t0 : t0 + TOK_TILE, j * IDX : (j + 1) * IDX]
                    for j in range(j0, j0 + HEAD_STEP)
                ],
                0,
            )
            prod = jnp.dot(lhs, keys_t, preferred_element_type=jnp.float32)
            for j in range(HEAD_STEP):
                weight = jnp.broadcast_to(
                    weights[t0 : t0 + TOK_TILE, j0 + j : j0 + j + 1], (TOK_TILE, LANES)
                )
                weight = jnp.concatenate([weight] * (width // LANES), 1)
                acc = acc + jnp.maximum(prod[j * TOK_TILE : (j + 1) * TOK_TILE], 0.0) * weight
        parts.append(acc)
    return jnp.concatenate(parts, 0)


def window_keys(keys_ref, tok, each, step):
    span = BLK + tok
    return jnp.concatenate(
        [
            keys_ref[pl.ds(pl.multiple_of((step * each + n) * span + BLK, BLK), tok), :]
            for n in range(each)
        ],
        0,
    )


def index_line_kernel(shards, iq_hbm, w_hbm, keys_ref, out_ref, iq_ref, w_ref, sem):
    tok = iq_ref.shape[0]
    each = TILE // tok
    w_copy = pltpu.make_async_copy(w_hbm, w_ref, sem.at[tok // TOK_TILE])
    w_copy.start()
    pieces = []
    for n in range(tok // TOK_TILE):
        part = pl.ds(n * TOK_TILE, TOK_TILE)
        pieces.append(pltpu.make_async_copy(iq_hbm.at[part], iq_ref.at[part], sem.at[n]))
        pieces[-1].start()
    w_copy.wait()
    weights = w_ref[...].T * IDX**-0.5
    value = index_tile(iq_ref, weights, window_keys(keys_ref, tok, each, 0), pieces)
    for n in range(each):
        out_ref[n] = value[:, n * tok : (n + 1) * tok]

    if shards > each:

        @pl.loop(1, shards // each)
        def _(step):
            value = index_tile(iq_ref, weights, window_keys(keys_ref, tok, each, step))
            for n in range(each):
                out_ref[step * each + n] = value[:, n * tok : (n + 1) * tok]


def index_window_kernel(shards, iq_ref, w_ref, keys_ref, out_ref):
    tok = iq_ref.shape[0]
    each = TILE // tok
    weights = w_ref[...].T * IDX**-0.5

    @pl.loop(0, shards // each)
    def _(step):
        value = index_tile(iq_ref, weights, window_keys(keys_ref, tok, each, step))
        for n in range(each):
            out_ref[step * each + n] = value[:, n * tok : (n + 1) * tok]


def index_prefix_kernel(places, *refs):
    count = len(places)
    own_ref, iq_ref, w_ref = refs[:3]
    key_refs, done_refs = refs[3 : 3 + count], refs[3 + count : 3 + 2 * count]
    prefix_ref, window_ref, keys_ref = refs[3 + 2 * count :]
    own = own_ref[0]
    tok = iq_ref.shape[0]
    span = BLK + tok
    weights = w_ref[...].T * IDX**-0.5
    for ref, rels in zip(key_refs, places):
        for n, rel in enumerate(rels):
            at = pl.multiple_of((own ^ rel) * BLK, BLK)
            keys_ref[pl.ds(at, BLK), :] = ref[n * span : n * span + BLK, :]
    row = lax.broadcasted_iota(jnp.int32, (tok, LANES), 0)
    lane = lax.broadcasted_iota(jnp.int32, (tok, LANES), 1)
    for ref, rels in zip(done_refs, places):
        for n, rel in enumerate(rels):
            other = own ^ rel
            seen = other * tok + lane <= own * tok + row
            window_ref[:, pl.ds(pl.multiple_of(other * tok, LANES), LANES)] = jnp.where(
                seen, ref[n], 0.0
            )

    @pl.loop(0, keys_ref.shape[0] // TILE)
    def _(step):
        at = pl.multiple_of(step * TILE, TILE)
        prefix_ref[:, pl.ds(at, TILE)] = index_tile(iq_ref, weights, keys_ref[pl.ds(at, TILE), :])


def attention_kernel(devices, own_ref, pick_ref, q_ref, *refs):
    shards = refs[:devices]
    out_ref, cache, raw, even_t, odd_t, need, sem = refs[devices:]
    block = pl.program_id(0)
    own = own_ref[0]
    picks = pick_ref.shape[1]

    def split(pick):
        window = pick - devices
        holder = jnp.where(window < 0, pick, window // 2)
        return holder ^ own, jnp.where(window < 0, 0, 1 + window % 2)

    def fetch(rel, inner, slot):
        return pltpu.make_async_copy(
            shards[rel].at[pl.ds(pl.multiple_of(inner * BLK, BLK), BLK)],
            cache.at[slot],
            sem.at[slot],
        )

    @pl.when((block == 0) & (pl.program_id(1) == 0))
    def _():
        for rel in range(devices):
            need[rel] = 0
        for b in range(pick_ref.shape[0]):
            for s in range(picks):
                rel, inner = split(pick_ref[b, s])
                need[rel] = inner
        for n in range(3):
            fetch(0, n, 0 if n == 0 else devices - 1 + n).start()
        for rel in range(1, devices):
            fetch(rel, need[rel], rel).start()
        for n in range(3):
            fetch(0, n, 0 if n == 0 else devices - 1 + n).wait()
        for rel in range(1, devices):
            fetch(rel, need[rel], rel).wait()

    @pl.when(pl.program_id(1) == 0)
    def _():
        own_pick = devices + own * 2 + block
        own_slot = jnp.int32(0)
        for s in range(picks):
            own_slot = jnp.where(pick_ref[block, s] == own_pick, s, own_slot)
        for s in range(picks):
            place = jnp.where(own_slot == s, picks - 1, own_slot if s == picks - 1 else s)
            rel, inner = split(pick_ref[block, s])
            slot = jnp.where((rel == 0) & (inner > 0), devices - 1 + inner, rel)
            raw[pl.ds(pl.multiple_of(place * BLK, BLK), BLK), :] = cache[slot]
        turned = raw[...].T
        even_t[...] = turned
        odd_t[0:ROPE] = turned[ROW:WIDE]
        odd_t[ROPE:WIDE] = turned[0:ROW]

    count = picks * BLK
    row = lax.broadcasted_iota(jnp.int32, (BLK, LANES), 0)
    lane = lax.broadcasted_iota(jnp.int32, (BLK, LANES), 1)
    allowed = jnp.concatenate([lane - BLK <= row] * GROUP, 0)

    def score(unit):
        odd, first = unit % 2, unit // 2 * GROUP
        lhs = jnp.concatenate(
            [
                q_ref[:, (first + g) * 2 * ROW + odd * LAT : (first + g) * 2 * ROW + odd * LAT + WIDE]
                for g in range(GROUP)
            ],
            0,
        )
        return jnp.dot(lhs, (odd_t if odd else even_t)[...], preferred_element_type=jnp.float32)

    def finish(unit, scores):
        odd, first = unit % 2, unit // 2 * GROUP
        last = jnp.where(allowed, scores[:, count - LANES :], LOW)
        scores = jnp.concatenate([scores[:, : count - LANES], last], 1)
        peak = jnp.max(scores, axis=1, keepdims=True)
        weights = jnp.exp2((scores - peak) * EXP2_SCALE)
        total = jnp.sum(weights, axis=1, keepdims=True)
        result = jnp.dot(
            weights.astype(jnp.bfloat16), raw[:, :LAT], preferred_element_type=jnp.float32
        )
        result = (result * (1.0 / total)).astype(jnp.bfloat16)
        for g in range(GROUP):
            at = (first + g) * 2 * LAT + odd * LAT
            out_ref[:, at : at + LAT] = result[g * BLK : (g + 1) * BLK]

    units = PAIRS // GROUP * 2
    scores = score(0)
    for unit in range(units):
        following = score(unit + 1) if unit + 1 < units else None
        finish(unit, scores)
        scores = following


def body(
    queries,
    prefix_latent,
    window_latent,
    index_queries,
    index_weights,
    prefix_index_keys,
    window_index_keys,
    picks,
):
    devices = lax.axis_size("ctx")
    own = lax.axis_index("ctx").astype(jnp.int32).reshape(1)
    tok = queries.shape[0]
    per_device = tok // BLK
    span = BLK + tok

    def swap(array, rel):
        return lax.ppermute(array, "ctx", [(i, i ^ rel) for i in range(devices)])

    smem = pl.BlockSpec(memory_space=pltpu.SMEM)
    vmem = pl.BlockSpec(memory_space=pltpu.VMEM)
    hbm = pl.BlockSpec(memory_space=pltpu.HBM)
    params = pltpu.CompilerParams(vmem_limit_bytes=VMEM)

    def index_cost(keys):
        return pl.CostEstimate(
            flops=2 * tok * IH * IDX * keys * 4, bytes_accessed=2**22, transcendentals=0
        )

    weights = index_weights.T

    def index_line(shard_keys):
        count = shard_keys.shape[0] // span
        return pl.pallas_call(
            functools.partial(index_line_kernel, count),
            out_shape=jax.ShapeDtypeStruct((count, tok, LANES), jnp.float32),
            in_specs=[hbm, hbm, vmem],
            out_specs=vmem,
            scratch_shapes=[
                pltpu.VMEM((tok, IH * IDX), jnp.bfloat16),
                pltpu.VMEM((IH, tok), jnp.float32),
                pltpu.SemaphoreType.DMA((tok // TOK_TILE + 1,)),
            ],
            compiler_params=params,
            cost_estimate=index_cost(count * tok),
        )(index_queries, weights, shard_keys)

    def index_window(shard_keys):
        count = shard_keys.shape[0] // span
        return pl.pallas_call(
            functools.partial(index_window_kernel, count),
            out_shape=jax.ShapeDtypeStruct((count, tok, LANES), jnp.float32),
            in_specs=[vmem, vmem, vmem],
            out_specs=vmem,
            compiler_params=params,
            cost_estimate=index_cost(count * tok),
        )(index_queries, weights, shard_keys)

    def after(done, *arrays):
        return lax.optimization_barrier((done, *arrays))[1:]

    bits = []
    bit = devices // 2
    while bit >= 4:
        bits.append(bit)
        bit //= 2

    low, high = bits[-1], bits[:-1]
    rows = jnp.concatenate([prefix_latent, window_latent], 0).reshape(3 * BLK, ROW)
    rows = jnp.pad(rows, ((0, 0), (0, WIDE - ROW)))
    shards = {0: rows}
    line, key_line = [0], jnp.concatenate([prefix_index_keys, window_index_keys], 0)
    (key_line,) = lax.optimization_barrier((key_line,))
    for bit in bits:
        other = swap(key_line, bit)
        if bit != low:
            (other, held) = lax.optimization_barrier((other, rows))
            shards[bit] = swap(held, bit)
        key_line = jnp.concatenate([key_line, other], 0)
        line = line + [rel ^ bit for rel in line]
    (held,) = after(key_line, rows)
    for bit in (low, 2):
        shards[bit] = swap(held, bit)
    key_side = swap(key_line, 2)
    side = [rel ^ 2 for rel in line]
    key_far = swap(jnp.concatenate([key_line, key_side], 0), 1)
    far = [rel ^ 1 for rel in line + side]

    def send(done, *moves):
        sources = sorted({rel for rel, _ in moves})
        held = dict(zip(sources, after(done, *[shards[rel] for rel in sources])))
        for rel, bit in moves:
            shards[rel ^ bit] = swap(held[rel], bit)

    line_done = index_line(key_line)
    send(line_done, (0, 1), (2, 1))
    side_done = index_window(key_side)
    send(side_done, (low, 2), (low, 1), *[(bit, 2) for bit in high], *[(bit, 1) for bit in high])
    rest = []
    for n, bit in enumerate(high):
        for other in bits[n + 1 :]:
            for rel in [r for r in [bit] + rest if not r & (2 * other - 1) and r & -r > other]:
                (held,) = after(side_done, shards[rel])
                shards[rel ^ other] = swap(held, other)
                rest.append(rel ^ other)
    far_done = index_window(key_far)
    send(
        far_done,
        (low | 2, 1),
        *[(bit | 2, 1) for bit in high],
        *[(rel, 2) for rel in rest],
        *[(rel, 1) for rel in rest],
    )

    prefix_index, window_index = pl.pallas_call(
        functools.partial(index_prefix_kernel, [line, side, far]),
        out_shape=(
            jax.ShapeDtypeStruct((tok, devices * BLK), jnp.float32),
            jax.ShapeDtypeStruct((tok, devices * tok), jnp.float32),
        ),
        in_specs=[smem] + [vmem] * 8,
        out_specs=(vmem, vmem),
        scratch_shapes=[pltpu.VMEM((devices * BLK, IDX), jnp.bfloat16)],
        compiler_params=params,
        cost_estimate=index_cost(devices * BLK),
    )(
        own,
        index_queries,
        weights,
        key_line,
        key_side,
        key_far,
        line_done,
        side_done,
        far_done,
    )
    send(prefix_index, *[(rel | 2, 1) for rel in rest])
    shards = [shards[rel] for rel in range(devices)]

    count = picks.shape[1] * BLK
    attention = pl.pallas_call(
        functools.partial(attention_kernel, devices),
        grid_spec=pltpu.PrefetchScalarGridSpec(
            num_scalar_prefetch=2,
            grid=(per_device, H // 2 // PAIRS),
            in_specs=[pl.BlockSpec((BLK, PAIRS * 2 * ROW), lambda b, h, *_: (b, h))]
            + [hbm] * devices,
            out_specs=pl.BlockSpec((BLK, PAIRS * 2 * LAT), lambda b, h, *_: (b, h)),
            scratch_shapes=[
                pltpu.VMEM((devices + 2, BLK, WIDE), jnp.bfloat16),
                pltpu.VMEM((count, WIDE), jnp.bfloat16),
                pltpu.VMEM((WIDE, count), jnp.bfloat16),
                pltpu.VMEM((WIDE, count), jnp.bfloat16),
                pltpu.SMEM((devices,), jnp.int32),
                pltpu.SemaphoreType.DMA((devices + 2,)),
            ],
        ),
        out_shape=jax.ShapeDtypeStruct((tok, H * LAT), jnp.bfloat16),
        compiler_params=params,
        cost_estimate=pl.CostEstimate(
            flops=2 * tok * H * count * (WIDE + LAT), bytes_accessed=2**24, transcendentals=0
        ),
    )(own, picks, queries, *shards)
    return (attention, prefix_index, window_index)


def solution(mesh):
    placed = P(("groups", "ctx"), None)
    return jax.shard_map(
        body,
        mesh=mesh,
        in_specs=(placed,) * 8,
        out_specs=(placed,) * 3,
        check_vma=False,
    )
```

```python
import functools

import jax
import jax.numpy as jnp
from jax import lax
from jax.experimental import pallas as pl
from jax.experimental.pallas import tpu as pltpu
from jax.sharding import PartitionSpec as P

H = 64
LAT = 512
ROPE = 64
ROW = LAT + ROPE
WIDE = 640
IH = 64
IDX = 128
BLK = 64
LANES = 128
TILE = 512
TOK_TILE = 32
HEAD_STEP = 16
PAIRS = 8
GROUP = 8
LOW = -1.0e30
EXP2_SCALE = 192.0**-0.5 * 1.4426950408889634
VMEM = 48 * 2**20
INDEX_VMEM = 60 * 2**20


def index_tile(iq_ref, weights, keys, pieces=None):
    keys_t = keys.T
    rows, width = iq_ref.shape[0], keys.shape[0]
    parts = []
    for t0 in range(0, rows, TOK_TILE):
        if pieces is not None:
            pieces[t0 // TOK_TILE].wait()
        acc = jnp.zeros((TOK_TILE, width), jnp.float32)
        for j0 in range(0, IH, HEAD_STEP):
            lhs = jnp.concatenate(
                [
                    iq_ref[t0 : t0 + TOK_TILE, j * IDX : (j + 1) * IDX]
                    for j in range(j0, j0 + HEAD_STEP)
                ],
                0,
            )
            prod = jnp.dot(lhs, keys_t, preferred_element_type=jnp.float32)
            for j in range(HEAD_STEP):
                weight = jnp.broadcast_to(
                    weights[t0 : t0 + TOK_TILE, j0 + j : j0 + j + 1], (TOK_TILE, LANES)
                )
                weight = jnp.concatenate([weight] * (width // LANES), 1)
                acc = acc + jnp.maximum(prod[j * TOK_TILE : (j + 1) * TOK_TILE], 0.0) * weight
        parts.append(acc)
    return jnp.concatenate(parts, 0)


def window_keys(keys_ref, tok, each, step):
    span = BLK + tok
    return jnp.concatenate(
        [
            keys_ref[pl.ds(pl.multiple_of((step * each + n) * span + BLK, BLK), tok), :]
            for n in range(each)
        ],
        0,
    )


def index_tiles(iq_hbm, w_hbm, iq_ref, w_ref, sem, steps, load, store, aside=None):
    tok = iq_ref.shape[0]
    w_copy = pltpu.make_async_copy(w_hbm, w_ref, sem.at[tok // TOK_TILE])
    w_copy.start()
    pieces = []
    for n in range(tok // TOK_TILE):
        part = pl.ds(n * TOK_TILE, TOK_TILE)
        pieces.append(pltpu.make_async_copy(iq_hbm.at[part], iq_ref.at[part], sem.at[n]))
        pieces[-1].start()
    if aside is not None:
        aside()
    w_copy.wait()
    weights = w_ref[...].T * IDX**-0.5
    store(0, index_tile(iq_ref, weights, load(0), pieces))
    if steps > 1:

        @pl.loop(1, steps)
        def _(step):
            store(step, index_tile(iq_ref, weights, load(step)))


def index_window_kernel(shards, iq_hbm, w_hbm, keys_ref, out_ref, iq_ref, w_ref, sem):
    tok = iq_ref.shape[0]
    each = TILE // tok

    def store(step, value):
        for n in range(each):
            out_ref[step * each + n] = value[:, n * tok : (n + 1) * tok]

    def load(step):
        return window_keys(keys_ref, tok, each, step)

    index_tiles(iq_hbm, w_hbm, iq_ref, w_ref, sem, shards // each, load, store)


def order_prefix(places, own, tok, key_refs, keys_ref):
    for ref, rels in zip(key_refs, places):
        for n, rel in enumerate(rels):
            at = pl.multiple_of((own ^ rel) * BLK, BLK)
            span = BLK + tok
            keys_ref[pl.ds(at, BLK), :] = ref[n * span : n * span + BLK, :]


def index_prefix_kernel(places, first, steps, own_ref, iq_hbm, w_hbm, *refs):
    count = len(places)
    out_ref, iq_ref, w_ref, sem, keys_ref = refs[count:]

    def aside():
        order_prefix(places, own_ref[0], iq_ref.shape[0], refs[:count], keys_ref)

    def load(step):
        return keys_ref[pl.ds(pl.multiple_of((first + step) * TILE, TILE), TILE), :]

    def store(step, value):
        out_ref[:, pl.ds(pl.multiple_of(step * TILE, TILE), TILE)] = value

    index_tiles(iq_hbm, w_hbm, iq_ref, w_ref, sem, steps, load, store, aside)


def index_last_kernel(places, first, steps, own_ref, iq_hbm, w_hbm, *refs):
    count = len(places)
    key_refs, done_refs = refs[:count], refs[count : 2 * count]
    begun_ref, prefix_ref, window_ref, iq_ref, w_ref, sem, keys_ref = refs[2 * count :]

    def aside():
        own = own_ref[0]
        tok = iq_ref.shape[0]
        order_prefix(places, own, tok, key_refs, keys_ref)
        prefix_ref[:, : first * TILE] = begun_ref[...]
        row = lax.broadcasted_iota(jnp.int32, (tok, LANES), 0)
        lane = lax.broadcasted_iota(jnp.int32, (tok, LANES), 1)
        for ref, rels in zip(done_refs, places):
            for n, rel in enumerate(rels):
                other = own ^ rel
                seen = other * tok + lane <= own * tok + row
                window_ref[:, pl.ds(pl.multiple_of(other * tok, LANES), LANES)] = jnp.where(
                    seen, ref[n], 0.0
                )

    def load(step):
        return keys_ref[pl.ds(pl.multiple_of((first + step) * TILE, TILE), TILE), :]

    def store(step, value):
        prefix_ref[:, pl.ds(pl.multiple_of((first + step) * TILE, TILE), TILE)] = value

    index_tiles(iq_hbm, w_hbm, iq_ref, w_ref, sem, steps, load, store, aside)


def attention_kernel(devices, own_ref, pick_ref, q_ref, *refs):
    shards = refs[:devices]
    out_ref, cache, raw, even_t, odd_t, need, sem = refs[devices:]
    block = pl.program_id(0)
    own = own_ref[0]
    picks = pick_ref.shape[1]

    def split(pick):
        window = pick - devices
        holder = jnp.where(window < 0, pick, window // 2)
        return holder ^ own, jnp.where(window < 0, 0, 1 + window % 2)

    def fetch(rel, inner, slot):
        return pltpu.make_async_copy(
            shards[rel].at[pl.ds(pl.multiple_of(inner * BLK, BLK), BLK)],
            cache.at[slot],
            sem.at[slot],
        )

    @pl.when((block == 0) & (pl.program_id(1) == 0))
    def _():
        for rel in range(devices):
            need[rel] = 0
        for b in range(pick_ref.shape[0]):
            for s in range(picks):
                rel, inner = split(pick_ref[b, s])
                need[rel] = inner
        for n in range(3):
            fetch(0, n, 0 if n == 0 else devices - 1 + n).start()
        for rel in range(1, devices):
            fetch(rel, need[rel], rel).start()
        for n in range(3):
            fetch(0, n, 0 if n == 0 else devices - 1 + n).wait()
        for rel in range(1, devices):
            fetch(rel, need[rel], rel).wait()

    @pl.when(pl.program_id(1) == 0)
    def _():
        own_pick = devices + own * 2 + block
        own_slot = jnp.int32(0)
        for s in range(picks):
            own_slot = jnp.where(pick_ref[block, s] == own_pick, s, own_slot)
        for s in range(picks):
            place = jnp.where(own_slot == s, picks - 1, own_slot if s == picks - 1 else s)
            rel, inner = split(pick_ref[block, s])
            slot = jnp.where((rel == 0) & (inner > 0), devices - 1 + inner, rel)
            raw[pl.ds(pl.multiple_of(place * BLK, BLK), BLK), :] = cache[slot]
        turned = raw[...].T
        even_t[...] = turned
        odd_t[0:ROPE] = turned[ROW:WIDE]
        odd_t[ROPE:WIDE] = turned[0:ROW]

    count = picks * BLK
    row = lax.broadcasted_iota(jnp.int32, (BLK, LANES), 0)
    lane = lax.broadcasted_iota(jnp.int32, (BLK, LANES), 1)
    allowed = jnp.concatenate([lane - BLK <= row] * GROUP, 0)

    def score(unit):
        odd, first = unit % 2, unit // 2 * GROUP
        lhs = jnp.concatenate(
            [
                q_ref[:, (first + g) * 2 * ROW + odd * LAT : (first + g) * 2 * ROW + odd * LAT + WIDE]
                for g in range(GROUP)
            ],
            0,
        )
        return jnp.dot(lhs, (odd_t if odd else even_t)[...], preferred_element_type=jnp.float32)

    def finish(unit, scores):
        odd, first = unit % 2, unit // 2 * GROUP
        last = jnp.where(allowed, scores[:, count - LANES :], LOW)
        scores = jnp.concatenate([scores[:, : count - LANES], last], 1)
        peak = jnp.max(scores, axis=1, keepdims=True)
        weights = jnp.exp2((scores - peak) * EXP2_SCALE)
        total = jnp.sum(weights, axis=1, keepdims=True)
        result = jnp.dot(
            weights.astype(jnp.bfloat16), raw[:, :LAT], preferred_element_type=jnp.float32
        )
        result = (result * (1.0 / total)).astype(jnp.bfloat16)
        for g in range(GROUP):
            at = (first + g) * 2 * LAT + odd * LAT
            out_ref[:, at : at + LAT] = result[g * BLK : (g + 1) * BLK]

    units = PAIRS // GROUP * 2
    scores = score(0)
    for unit in range(units):
        following = score(unit + 1) if unit + 1 < units else None
        finish(unit, scores)
        scores = following


def body(
    queries,
    prefix_latent,
    window_latent,
    index_queries,
    index_weights,
    prefix_index_keys,
    window_index_keys,
    picks,
):
    devices = lax.axis_size("ctx")
    own = lax.axis_index("ctx").astype(jnp.int32).reshape(1)
    tok = queries.shape[0]
    per_device = tok // BLK
    span = BLK + tok

    def swap(array, rel):
        return lax.ppermute(array, "ctx", [(i, i ^ rel) for i in range(devices)])

    smem = pl.BlockSpec(memory_space=pltpu.SMEM)
    vmem = pl.BlockSpec(memory_space=pltpu.VMEM)
    hbm = pl.BlockSpec(memory_space=pltpu.HBM)
    params = pltpu.CompilerParams(vmem_limit_bytes=VMEM)

    def index_cost(keys):
        return pl.CostEstimate(
            flops=2 * tok * IH * IDX * keys * 4, bytes_accessed=2**22, transcendentals=0
        )

    weights = index_weights.T

    index_scratch = [
        pltpu.VMEM((tok, IH * IDX), jnp.bfloat16),
        pltpu.VMEM((IH, tok), jnp.float32),
        pltpu.SemaphoreType.DMA((tok // TOK_TILE + 1,)),
    ]
    order_scratch = [pltpu.VMEM((devices * BLK, IDX), jnp.bfloat16)]
    index_params = pltpu.CompilerParams(vmem_limit_bytes=INDEX_VMEM)

    def index_window(shard_keys):
        count = shard_keys.shape[0] // span
        return pl.pallas_call(
            functools.partial(index_window_kernel, count),
            out_shape=jax.ShapeDtypeStruct((count, tok, LANES), jnp.float32),
            in_specs=[hbm, hbm, vmem],
            out_specs=vmem,
            scratch_shapes=index_scratch,
            compiler_params=index_params,
            cost_estimate=index_cost(count * tok),
        )(index_queries, weights, shard_keys)

    def after(done, *arrays):
        return lax.optimization_barrier((done, *arrays))[1:]

    bits = []
    bit = devices // 2
    while bit >= 4:
        bits.append(bit)
        bit //= 2

    low, high = bits[-1], bits[:-1]
    rows = jnp.concatenate([prefix_latent, window_latent], 0).reshape(3 * BLK, ROW)
    rows = jnp.pad(rows, ((0, 0), (0, WIDE - ROW)))
    shards = {0: rows}
    line, key_line = [0], jnp.concatenate([prefix_index_keys, window_index_keys], 0)
    (key_line,) = lax.optimization_barrier((key_line,))
    for bit in bits:
        other = swap(key_line, bit)
        if bit != low:
            (other, held) = lax.optimization_barrier((other, rows))
            shards[bit] = swap(held, bit)
        key_line = jnp.concatenate([key_line, other], 0)
        line = line + [rel ^ bit for rel in line]
    (held,) = after(key_line, rows)
    for bit in (low, 2):
        shards[bit] = swap(held, bit)
    key_side = swap(key_line, 2)
    side = [rel ^ 2 for rel in line]
    key_far = swap(jnp.concatenate([key_line, key_side], 0), 1)
    far = [rel ^ 1 for rel in line + side]

    def send(done, *moves):
        sources = sorted({rel for rel, _ in moves})
        held = dict(zip(sources, after(done, *[shards[rel] for rel in sources])))
        for rel, bit in moves:
            shards[rel ^ bit] = swap(held[rel], bit)

    line_done = index_window(key_line)
    send(line_done, (0, 1))
    def settle(array, done, rels):
        got = lax.optimization_barrier((array, done, *[shards[rel] for rel in rels]))
        shards.update(zip(rels, got[2:]))
        return got[0]

    side_done = index_window(key_side)
    side_done = settle(side_done, weights, [1, 2])
    send(side_done, (low, 2), (low, 1), *[(bit, 2) for bit in high], *[(bit, 1) for bit in high])
    rest = []
    for n, bit in enumerate(high):
        for other in bits[n + 1 :]:
            for rel in [r for r in [bit] + rest if not r & (2 * other - 1) and r & -r > other]:
                (held,) = after(side_done, shards[rel])
                shards[rel ^ other] = swap(held, other)
                rest.append(rel ^ other)
    far_done = index_window(key_far)
    send(far_done, *[(rel, 2) for rel in rest], *[(rel, 1) for rel in rest], (2, 1))
    held = settle(index_queries, far_done, [rel ^ 1 for rel in bits] + rest)
    places = [line, side, far]
    tiles = devices * BLK // TILE
    begun = pl.pallas_call(
        functools.partial(index_prefix_kernel, places, 0, tiles // 2),
        out_shape=jax.ShapeDtypeStruct((tok, tiles // 2 * TILE), jnp.float32),
        in_specs=[smem, hbm, hbm, vmem, vmem, vmem],
        out_specs=vmem,
        scratch_shapes=index_scratch + order_scratch,
        compiler_params=index_params,
        cost_estimate=index_cost(tiles // 2 * TILE),
    )(own, held, weights, key_line, key_side, key_far)
    send(begun, (low | 2, 1), *[(bit | 2, 1) for bit in high])
    held = settle(index_queries, begun, [rel ^ 1 for rel in rest] + [3] + [rel | 2 for rel in bits])
    prefix_index, window_index = pl.pallas_call(
        functools.partial(index_last_kernel, places, tiles // 2, tiles - tiles // 2),
        out_shape=(
            jax.ShapeDtypeStruct((tok, devices * BLK), jnp.float32),
            jax.ShapeDtypeStruct((tok, devices * tok), jnp.float32),
        ),
        in_specs=[smem, hbm, hbm] + [vmem] * 7,
        out_specs=(vmem, vmem),
        scratch_shapes=index_scratch + order_scratch,
        compiler_params=index_params,
        cost_estimate=index_cost(tiles // 2 * TILE),
    )(
        own,
        held,
        weights,
        key_line,
        key_side,
        key_far,
        line_done,
        side_done,
        far_done,
        begun,
    )
    send(prefix_index, *[(rel | 2, 1) for rel in rest])
    shards = [shards[rel] for rel in range(devices)]

    count = picks.shape[1] * BLK
    attention = pl.pallas_call(
        functools.partial(attention_kernel, devices),
        grid_spec=pltpu.PrefetchScalarGridSpec(
            num_scalar_prefetch=2,
            grid=(per_device, H // 2 // PAIRS),
            in_specs=[pl.BlockSpec((BLK, PAIRS * 2 * ROW), lambda b, h, *_: (b, h))]
            + [hbm] * devices,
            out_specs=pl.BlockSpec((BLK, PAIRS * 2 * LAT), lambda b, h, *_: (b, h)),
            scratch_shapes=[
                pltpu.VMEM((devices + 2, BLK, WIDE), jnp.bfloat16),
                pltpu.VMEM((count, WIDE), jnp.bfloat16),
                pltpu.VMEM((WIDE, count), jnp.bfloat16),
                pltpu.VMEM((WIDE, count), jnp.bfloat16),
                pltpu.SMEM((devices,), jnp.int32),
                pltpu.SemaphoreType.DMA((devices + 2,)),
            ],
        ),
        out_shape=jax.ShapeDtypeStruct((tok, H * LAT), jnp.bfloat16),
        compiler_params=params,
        cost_estimate=pl.CostEstimate(
            flops=2 * tok * H * count * (WIDE + LAT), bytes_accessed=2**24, transcendentals=0
        ),
    )(own, picks, queries, *shards)
    return (attention, prefix_index, window_index)


def solution(mesh):
    placed = P(("groups", "ctx"), None)
    return jax.shard_map(
        body,
        mesh=mesh,
        in_specs=(placed,) * 8,
        out_specs=(placed,) * 3,
        check_vma=False,
    )
```

```python
import functools

import jax
import jax.numpy as jnp
from jax import lax
from jax.experimental import pallas as pl
from jax.experimental.pallas import tpu as pltpu
from jax.sharding import PartitionSpec as P

H = 64
LAT = 512
ROPE = 64
ROW = LAT + ROPE
WIDE = 640
IH = 64
IDX = 128
BLK = 64
LANES = 128
TILE = 512
TOK_TILE = 32
HEAD_STEP = 16
PAIRS = 8
GROUP = 8
LOW = -1.0e30
EXP2_SCALE = 192.0**-0.5 * 1.4426950408889634
VMEM = 48 * 2**20


def index_tile(iq_ref, weights, keys):
    keys_t = keys.T
    rows, width = iq_ref.shape[0], keys.shape[0]
    parts = []
    for t0 in range(0, rows, TOK_TILE):
        acc = jnp.zeros((TOK_TILE, width), jnp.float32)
        for j0 in range(0, IH, HEAD_STEP):
            lhs = jnp.concatenate(
                [
                    iq_ref[t0 : t0 + TOK_TILE, j * IDX : (j + 1) * IDX]
                    for j in range(j0, j0 + HEAD_STEP)
                ],
                0,
            )
            prod = jnp.dot(lhs, keys_t, preferred_element_type=jnp.float32)
            for j in range(HEAD_STEP):
                weight = jnp.broadcast_to(
                    weights[t0 : t0 + TOK_TILE, j0 + j : j0 + j + 1], (TOK_TILE, LANES)
                )
                weight = jnp.concatenate([weight] * (width // LANES), 1)
                acc = acc + jnp.maximum(prod[j * TOK_TILE : (j + 1) * TOK_TILE], 0.0) * weight
        parts.append(acc)
    return jnp.concatenate(parts, 0)


def window_keys(keys_ref, tok, each, step):
    span = BLK + tok
    return jnp.concatenate(
        [
            keys_ref[pl.ds(pl.multiple_of((step * each + n) * span + BLK, BLK), tok), :]
            for n in range(each)
        ],
        0,
    )


def weights_kernel(iq_ref, w_ref, out_ref):
    out_ref[...] = w_ref[...].T * IDX**-0.5


def index_tiles(iq_ref, w_ref, steps, load, store):
    weights = w_ref[...]

    @pl.loop(0, steps)
    def _(step):
        store(step, index_tile(iq_ref, weights, load(step)))


def index_window_kernel(shards, iq_ref, w_ref, keys_ref, out_ref):
    tok = iq_ref.shape[0]
    each = TILE // tok

    def store(step, value):
        for n in range(each):
            out_ref[step * each + n] = value[:, n * tok : (n + 1) * tok]

    def load(step):
        return window_keys(keys_ref, tok, each, step)

    index_tiles(iq_ref, w_ref, shards // each, load, store)


def order_prefix(places, own, tok, key_refs, keys_ref):
    for ref, rels in zip(key_refs, places):
        for n, rel in enumerate(rels):
            at = pl.multiple_of((own ^ rel) * BLK, BLK)
            span = BLK + tok
            keys_ref[pl.ds(at, BLK), :] = ref[n * span : n * span + BLK, :]


def index_prefix_kernel(places, first, steps, own_ref, iq_ref, w_ref, *refs):
    count = len(places)
    out_ref, keys_ref = refs[count:]
    order_prefix(places, own_ref[0], iq_ref.shape[0], refs[:count], keys_ref)

    def load(step):
        return keys_ref[pl.ds(pl.multiple_of((first + step) * TILE, TILE), TILE), :]

    def store(step, value):
        out_ref[:, pl.ds(pl.multiple_of(step * TILE, TILE), TILE)] = value

    index_tiles(iq_ref, w_ref, steps, load, store)


def index_last_kernel(places, first, steps, own_ref, iq_ref, w_ref, *refs):
    count = len(places)
    key_refs, done_refs = refs[:count], refs[count : 2 * count]
    begun_ref, prefix_ref, window_ref, keys_ref = refs[2 * count :]
    own = own_ref[0]
    tok = iq_ref.shape[0]
    order_prefix(places, own, tok, key_refs, keys_ref)
    prefix_ref[:, : first * TILE] = begun_ref[...]
    row = lax.broadcasted_iota(jnp.int32, (tok, LANES), 0)
    lane = lax.broadcasted_iota(jnp.int32, (tok, LANES), 1)
    for ref, rels in zip(done_refs, places):
        for n, rel in enumerate(rels):
            other = own ^ rel
            seen = other * tok + lane <= own * tok + row
            window_ref[:, pl.ds(pl.multiple_of(other * tok, LANES), LANES)] = jnp.where(
                seen, ref[n], 0.0
            )

    def load(step):
        return keys_ref[pl.ds(pl.multiple_of((first + step) * TILE, TILE), TILE), :]

    def store(step, value):
        prefix_ref[:, pl.ds(pl.multiple_of((first + step) * TILE, TILE), TILE)] = value

    index_tiles(iq_ref, w_ref, steps, load, store)


def attention_kernel(devices, own_ref, pick_ref, q_ref, *refs):
    shards = refs[:devices]
    out_ref, cache, raw, even_t, odd_t, need, sem = refs[devices:]
    block = pl.program_id(0)
    own = own_ref[0]
    picks = pick_ref.shape[1]

    def split(pick):
        window = pick - devices
        holder = jnp.where(window < 0, pick, window // 2)
        return holder ^ own, jnp.where(window < 0, 0, 1 + window % 2)

    def fetch(rel, inner, slot):
        return pltpu.make_async_copy(
            shards[rel].at[pl.ds(pl.multiple_of(inner * BLK, BLK), BLK)],
            cache.at[slot],
            sem.at[slot],
        )

    @pl.when((block == 0) & (pl.program_id(1) == 0))
    def _():
        for rel in range(devices):
            need[rel] = 0
        for b in range(pick_ref.shape[0]):
            for s in range(picks):
                rel, inner = split(pick_ref[b, s])
                need[rel] = inner
        for n in range(3):
            fetch(0, n, 0 if n == 0 else devices - 1 + n).start()
        for rel in range(1, devices):
            fetch(rel, need[rel], rel).start()
        for n in range(3):
            fetch(0, n, 0 if n == 0 else devices - 1 + n).wait()
        for rel in range(1, devices):
            fetch(rel, need[rel], rel).wait()

    @pl.when(pl.program_id(1) == 0)
    def _():
        own_pick = devices + own * 2 + block
        own_slot = jnp.int32(0)
        for s in range(picks):
            own_slot = jnp.where(pick_ref[block, s] == own_pick, s, own_slot)
        for s in range(picks):
            place = jnp.where(own_slot == s, picks - 1, own_slot if s == picks - 1 else s)
            rel, inner = split(pick_ref[block, s])
            slot = jnp.where((rel == 0) & (inner > 0), devices - 1 + inner, rel)
            raw[pl.ds(pl.multiple_of(place * BLK, BLK), BLK), :] = cache[slot]
        turned = raw[...].T
        even_t[...] = turned
        odd_t[0:ROPE] = turned[ROW:WIDE]
        odd_t[ROPE:WIDE] = turned[0:ROW]

    count = picks * BLK
    row = lax.broadcasted_iota(jnp.int32, (BLK, LANES), 0)
    lane = lax.broadcasted_iota(jnp.int32, (BLK, LANES), 1)
    allowed = jnp.concatenate([lane - BLK <= row] * GROUP, 0)

    def score(unit):
        odd, first = unit % 2, unit // 2 * GROUP
        lhs = jnp.concatenate(
            [
                q_ref[:, (first + g) * 2 * ROW + odd * LAT : (first + g) * 2 * ROW + odd * LAT + WIDE]
                for g in range(GROUP)
            ],
            0,
        )
        return jnp.dot(lhs, (odd_t if odd else even_t)[...], preferred_element_type=jnp.float32)

    def finish(unit, scores):
        odd, first = unit % 2, unit // 2 * GROUP
        last = jnp.where(allowed, scores[:, count - LANES :], LOW)
        scores = jnp.concatenate([scores[:, : count - LANES], last], 1)
        peak = jnp.max(scores, axis=1, keepdims=True)
        weights = jnp.exp2((scores - peak) * EXP2_SCALE)
        total = jnp.sum(weights, axis=1, keepdims=True)
        result = jnp.dot(
            weights.astype(jnp.bfloat16), raw[:, :LAT], preferred_element_type=jnp.float32
        )
        result = (result * (1.0 / total)).astype(jnp.bfloat16)
        for g in range(GROUP):
            at = (first + g) * 2 * LAT + odd * LAT
            out_ref[:, at : at + LAT] = result[g * BLK : (g + 1) * BLK]

    units = PAIRS // GROUP * 2
    scores = score(0)
    for unit in range(units):
        following = score(unit + 1) if unit + 1 < units else None
        finish(unit, scores)
        scores = following


def body(
    queries,
    prefix_latent,
    window_latent,
    index_queries,
    index_weights,
    prefix_index_keys,
    window_index_keys,
    picks,
):
    devices = lax.axis_size("ctx")
    own = lax.axis_index("ctx").astype(jnp.int32).reshape(1)
    tok = queries.shape[0]
    per_device = tok // BLK
    span = BLK + tok

    def swap(array, rel):
        return lax.ppermute(array, "ctx", [(i, i ^ rel) for i in range(devices)])

    smem = pl.BlockSpec(memory_space=pltpu.SMEM)
    vmem = pl.BlockSpec(memory_space=pltpu.VMEM)
    hbm = pl.BlockSpec(memory_space=pltpu.HBM)
    params = pltpu.CompilerParams(vmem_limit_bytes=VMEM)

    def index_cost(keys):
        return pl.CostEstimate(
            flops=2 * tok * IH * IDX * keys * 4, bytes_accessed=2**22, transcendentals=0
        )

    order_scratch = [pltpu.VMEM((devices * BLK, IDX), jnp.bfloat16)]

    def index_window(shard_keys):
        count = shard_keys.shape[0] // span
        return pl.pallas_call(
            functools.partial(index_window_kernel, count),
            out_shape=jax.ShapeDtypeStruct((count, tok, LANES), jnp.float32),
            in_specs=[vmem, vmem, vmem],
            out_specs=vmem,
            compiler_params=params,
            cost_estimate=index_cost(count * tok),
        )(index_queries, weights, shard_keys)

    def after(done, *arrays):
        return lax.optimization_barrier((done, *arrays))[1:]

    bits = []
    bit = devices // 2
    while bit >= 4:
        bits.append(bit)
        bit //= 2

    low, high = bits[-1], bits[:-1]
    rows = jnp.concatenate([prefix_latent, window_latent], 0).reshape(3 * BLK, ROW)
    rows = jnp.pad(rows, ((0, 0), (0, WIDE - ROW)))
    shards = {0: rows}
    line, key_line = [0], jnp.concatenate([prefix_index_keys, window_index_keys], 0)
    (key_line,) = lax.optimization_barrier((key_line,))
    for bit in bits:
        other = swap(key_line, bit)
        if bit != low:
            (other, held) = lax.optimization_barrier((other, rows))
            shards[bit] = swap(held, bit)
        key_line = jnp.concatenate([key_line, other], 0)
        line = line + [rel ^ bit for rel in line]
        if bit != low:
            touch_on = key_line
    (early_queries, early_weights) = after(touch_on, index_queries, index_weights.T)
    weights = pl.pallas_call(
        weights_kernel,
        out_shape=jax.ShapeDtypeStruct((tok, IH), jnp.float32),
        in_specs=[vmem, vmem],
        out_specs=vmem,
        compiler_params=params,
    )(early_queries, early_weights)
    (held,) = after(key_line, rows)
    for bit in (low, 2):
        shards[bit] = swap(held, bit)
    key_side = swap(key_line, 2)
    side = [rel ^ 2 for rel in line]
    key_far = swap(jnp.concatenate([key_line, key_side], 0), 1)
    far = [rel ^ 1 for rel in line + side]

    def send(done, *moves):
        sources = sorted({rel for rel, _ in moves})
        held = dict(zip(sources, after(done, *[shards[rel] for rel in sources])))
        for rel, bit in moves:
            shards[rel ^ bit] = swap(held[rel], bit)

    line_done = index_window(key_line)
    send(line_done, (0, 1))
    def settle(array, done, rels):
        got = lax.optimization_barrier((array, done, *[shards[rel] for rel in rels]))
        shards.update(zip(rels, got[2:]))
        return got[0]

    side_done = index_window(key_side)
    side_done = settle(side_done, weights, [1, 2])
    send(side_done, (low, 2), (low, 1), *[(bit, 2) for bit in high], *[(bit, 1) for bit in high])
    rest = []
    for n, bit in enumerate(high):
        for other in bits[n + 1 :]:
            for rel in [r for r in [bit] + rest if not r & (2 * other - 1) and r & -r > other]:
                (held,) = after(side_done, shards[rel])
                shards[rel ^ other] = swap(held, other)
                rest.append(rel ^ other)
    far_done = index_window(key_far)
    send(far_done, *[(rel, 2) for rel in rest], *[(rel, 1) for rel in rest], (2, 1))
    held = settle(index_queries, far_done, [rel ^ 1 for rel in bits] + rest)
    places = [line, side, far]
    tiles = devices * BLK // TILE
    begun = pl.pallas_call(
        functools.partial(index_prefix_kernel, places, 0, tiles // 2),
        out_shape=jax.ShapeDtypeStruct((tok, tiles // 2 * TILE), jnp.float32),
        in_specs=[smem] + [vmem] * 5,
        out_specs=vmem,
        scratch_shapes=order_scratch,
        compiler_params=params,
        cost_estimate=index_cost(tiles // 2 * TILE),
    )(own, held, weights, key_line, key_side, key_far)
    send(begun, (low | 2, 1), *[(bit | 2, 1) for bit in high])
    held = settle(index_queries, begun, [rel ^ 1 for rel in rest] + [3] + [rel | 2 for rel in bits])
    prefix_index, window_index = pl.pallas_call(
        functools.partial(index_last_kernel, places, tiles // 2, tiles - tiles // 2),
        out_shape=(
            jax.ShapeDtypeStruct((tok, devices * BLK), jnp.float32),
            jax.ShapeDtypeStruct((tok, devices * tok), jnp.float32),
        ),
        in_specs=[smem] + [vmem] * 9,
        out_specs=(vmem, vmem),
        scratch_shapes=order_scratch,
        compiler_params=params,
        cost_estimate=index_cost(tiles // 2 * TILE),
    )(
        own,
        held,
        weights,
        key_line,
        key_side,
        key_far,
        line_done,
        side_done,
        far_done,
        begun,
    )
    send(prefix_index, *[(rel | 2, 1) for rel in rest])
    shards = [shards[rel] for rel in range(devices)]

    count = picks.shape[1] * BLK
    attention = pl.pallas_call(
        functools.partial(attention_kernel, devices),
        grid_spec=pltpu.PrefetchScalarGridSpec(
            num_scalar_prefetch=2,
            grid=(per_device, H // 2 // PAIRS),
            in_specs=[pl.BlockSpec((BLK, PAIRS * 2 * ROW), lambda b, h, *_: (b, h))]
            + [hbm] * devices,
            out_specs=pl.BlockSpec((BLK, PAIRS * 2 * LAT), lambda b, h, *_: (b, h)),
            scratch_shapes=[
                pltpu.VMEM((devices + 2, BLK, WIDE), jnp.bfloat16),
                pltpu.VMEM((count, WIDE), jnp.bfloat16),
                pltpu.VMEM((WIDE, count), jnp.bfloat16),
                pltpu.VMEM((WIDE, count), jnp.bfloat16),
                pltpu.SMEM((devices,), jnp.int32),
                pltpu.SemaphoreType.DMA((devices + 2,)),
            ],
        ),
        out_shape=jax.ShapeDtypeStruct((tok, H * LAT), jnp.bfloat16),
        compiler_params=params,
        cost_estimate=pl.CostEstimate(
            flops=2 * tok * H * count * (WIDE + LAT), bytes_accessed=2**24, transcendentals=0
        ),
    )(own, picks, queries, *shards)
    return (attention, prefix_index, window_index)


def solution(mesh):
    placed = P(("groups", "ctx"), None)
    return jax.shard_map(
        body,
        mesh=mesh,
        in_specs=(placed,) * 8,
        out_specs=(placed,) * 3,
        check_vma=False,
    )
```

```python
import functools

import jax
import jax.numpy as jnp
from jax import lax
from jax.experimental import pallas as pl
from jax.experimental.pallas import tpu as pltpu
from jax.sharding import PartitionSpec as P

H = 64
LAT = 512
ROPE = 64
ROW = LAT + ROPE
WIDE = 640
IH = 64
IDX = 128
BLK = 64
LANES = 128
TILE = 512
TOK_TILE = 32
HEAD_STEP = 16
PAIRS = 8
GROUP = 8
LOW = -1.0e30
EXP2_SCALE = 192.0**-0.5 * 1.4426950408889634
VMEM = 48 * 2**20


def index_tile(iq_ref, weights, keys):
    keys_t = keys.T
    rows, width = iq_ref.shape[0], keys.shape[0]
    parts = []
    for t0 in range(0, rows, TOK_TILE):
        acc = jnp.zeros((TOK_TILE, width), jnp.float32)
        for j0 in range(0, IH, HEAD_STEP):
            lhs = jnp.concatenate(
                [
                    iq_ref[t0 : t0 + TOK_TILE, j * IDX : (j + 1) * IDX]
                    for j in range(j0, j0 + HEAD_STEP)
                ],
                0,
            )
            prod = jnp.dot(lhs, keys_t, preferred_element_type=jnp.float32)
            for j in range(HEAD_STEP):
                weight = jnp.broadcast_to(
                    weights[t0 : t0 + TOK_TILE, j0 + j : j0 + j + 1], (TOK_TILE, LANES)
                )
                weight = jnp.concatenate([weight] * (width // LANES), 1)
                acc = acc + jnp.maximum(prod[j * TOK_TILE : (j + 1) * TOK_TILE], 0.0) * weight
        parts.append(acc)
    return jnp.concatenate(parts, 0)


def window_keys(keys_ref, tok, each, step):
    span = BLK + tok
    return jnp.concatenate(
        [
            keys_ref[pl.ds(pl.multiple_of((step * each + n) * span + BLK, BLK), tok), :]
            for n in range(each)
        ],
        0,
    )


def weights_kernel(iq_ref, w_ref, out_ref):
    out_ref[...] = w_ref[...].T * IDX**-0.5


def index_tiles(iq_ref, w_ref, steps, load, store):
    weights = w_ref[...]

    @pl.loop(0, steps)
    def _(step):
        store(step, index_tile(iq_ref, weights, load(step)))


def index_window_kernel(shards, iq_ref, w_ref, keys_ref, out_ref):
    tok = iq_ref.shape[0]
    each = TILE // tok

    def store(step, value):
        for n in range(each):
            out_ref[step * each + n] = value[:, n * tok : (n + 1) * tok]

    def load(step):
        return window_keys(keys_ref, tok, each, step)

    index_tiles(iq_ref, w_ref, shards // each, load, store)


def order_prefix(places, own, tok, key_refs, keys_ref):
    for ref, rels in zip(key_refs, places):
        for n, rel in enumerate(rels):
            at = pl.multiple_of((own ^ rel) * BLK, BLK)
            span = BLK + tok
            keys_ref[pl.ds(at, BLK), :] = ref[n * span : n * span + BLK, :]


def index_prefix_kernel(places, first, steps, own_ref, iq_ref, w_ref, *refs):
    count = len(places)
    out_ref, keys_ref = refs[count:]
    order_prefix(places, own_ref[0], iq_ref.shape[0], refs[:count], keys_ref)

    def load(step):
        return keys_ref[pl.ds(pl.multiple_of((first + step) * TILE, TILE), TILE), :]

    def store(step, value):
        out_ref[:, pl.ds(pl.multiple_of(step * TILE, TILE), TILE)] = value

    index_tiles(iq_ref, w_ref, steps, load, store)


def split_pick(pick, devices, own):
    window = pick - devices
    holder = jnp.where(window < 0, pick, window // 2)
    return holder ^ own, jnp.where(window < 0, 0, 1 + window % 2)


def find_blocks(need, pick_ref, devices, own):
    for rel in range(devices):
        need[rel] = 0
    for b in range(pick_ref.shape[0]):
        for s in range(pick_ref.shape[1]):
            rel, inner = split_pick(pick_ref[b, s], devices, own)
            need[rel] = inner


def block_copy(shard, inner, target, sem):
    return pltpu.make_async_copy(
        shard.at[pl.ds(pl.multiple_of(inner * BLK, BLK), BLK)], target, sem
    )


def index_last_kernel(places, early, first, steps, own_ref, pick_ref, iq_ref, w_ref, *refs):
    count = len(places)
    key_refs, done_refs = refs[:count], refs[count : 2 * count]
    begun_ref, shards = refs[2 * count], refs[2 * count + 1 : 2 * count + 1 + len(early)]
    rest = refs[2 * count + 1 + len(early) :]
    prefix_hbm, window_hbm, cache, keys_ref, prefix_ref, window_ref, need, sem = rest
    own = own_ref[0]
    tok = iq_ref.shape[0]
    devices = prefix_ref.shape[1] // BLK
    find_blocks(need, pick_ref, devices, own)
    copies = []
    for n, rel in enumerate(early):
        if rel:
            copies.append(block_copy(shards[n], need[rel], cache.at[n], sem.at[n]))
        else:
            slots = [n, len(early), len(early) + 1]
            copies += [
                block_copy(shards[n], inner, cache.at[slot], sem.at[slot])
                for inner, slot in enumerate(slots)
            ]
    for copy in copies:
        copy.start()
    order_prefix(places, own, tok, key_refs, keys_ref)
    row = lax.broadcasted_iota(jnp.int32, (tok, LANES), 0)
    lane = lax.broadcasted_iota(jnp.int32, (tok, LANES), 1)
    for ref, rels in zip(done_refs, places):
        for n, rel in enumerate(rels):
            other = own ^ rel
            seen = other * tok + lane <= own * tok + row
            window_ref[:, pl.ds(pl.multiple_of(other * tok, LANES), LANES)] = jnp.where(
                seen, ref[n], 0.0
            )
    prefix_ref[:, : first * TILE] = begun_ref[...]
    window_out = pltpu.make_async_copy(window_ref, window_hbm, sem.at[len(early) + 2])
    window_out.start()

    def load(step):
        return keys_ref[pl.ds(pl.multiple_of((first + step) * TILE, TILE), TILE), :]

    def store(step, value):
        prefix_ref[:, pl.ds(pl.multiple_of((first + step) * TILE, TILE), TILE)] = value

    index_tiles(iq_ref, w_ref, steps, load, store)
    prefix_out = pltpu.make_async_copy(prefix_ref, prefix_hbm, sem.at[len(early) + 3])
    prefix_out.start()
    for copy in copies:
        copy.wait()
    window_out.wait()
    prefix_out.wait()


def attention_kernel(early, late, own_ref, pick_ref, q_ref, cache, *refs):
    shards = refs[: len(late)]
    out_ref, fetched, raw, even_t, odd_t, need, slot_of, sem = refs[len(late) :]
    block = pl.program_id(0)
    own = own_ref[0]
    picks = pick_ref.shape[1]
    devices = len(early) + len(late)

    @pl.when((block == 0) & (pl.program_id(1) == 0))
    def _():
        find_blocks(need, pick_ref, devices, own)
        copies = [
            block_copy(shards[n], need[rel], fetched.at[n], sem.at[n])
            for n, rel in enumerate(late)
        ]
        for copy in copies:
            copy.start()
        for n, rel in enumerate(early):
            slot_of[rel] = n
        for n, rel in enumerate(late):
            slot_of[rel] = len(early) + 2 + n
        for copy in copies:
            copy.wait()

    @pl.when(pl.program_id(1) == 0)
    def _():
        own_pick = devices + own * 2 + block
        own_slot = jnp.int32(0)
        for s in range(picks):
            own_slot = jnp.where(pick_ref[block, s] == own_pick, s, own_slot)
        for s in range(picks):
            place = jnp.where(own_slot == s, picks - 1, own_slot if s == picks - 1 else s)
            rel, inner = split_pick(pick_ref[block, s], devices, own)
            slot = jnp.where((rel == 0) & (inner > 0), len(early) - 1 + inner, slot_of[rel])
            rows = pl.ds(pl.multiple_of(place * BLK, BLK), BLK)

            @pl.when(slot < len(early) + 2)
            def _():
                raw[rows, :] = cache[slot]

            @pl.when(slot >= len(early) + 2)
            def _():
                raw[rows, :] = fetched[slot - (len(early) + 2)]

        turned = raw[...].T
        even_t[...] = turned
        odd_t[0:ROPE] = turned[ROW:WIDE]
        odd_t[ROPE:WIDE] = turned[0:ROW]

    count = picks * BLK
    row = lax.broadcasted_iota(jnp.int32, (BLK, LANES), 0)
    lane = lax.broadcasted_iota(jnp.int32, (BLK, LANES), 1)
    allowed = jnp.concatenate([lane - BLK <= row] * GROUP, 0)

    def score(unit):
        odd, first = unit % 2, unit // 2 * GROUP
        lhs = jnp.concatenate(
            [
                q_ref[:, (first + g) * 2 * ROW + odd * LAT : (first + g) * 2 * ROW + odd * LAT + WIDE]
                for g in range(GROUP)
            ],
            0,
        )
        return jnp.dot(lhs, (odd_t if odd else even_t)[...], preferred_element_type=jnp.float32)

    def finish(unit, scores):
        odd, first = unit % 2, unit // 2 * GROUP
        last = jnp.where(allowed, scores[:, count - LANES :], LOW)
        scores = jnp.concatenate([scores[:, : count - LANES], last], 1)
        peak = jnp.max(scores, axis=1, keepdims=True)
        weights = jnp.exp2((scores - peak) * EXP2_SCALE)
        total = jnp.sum(weights, axis=1, keepdims=True)
        result = jnp.dot(
            weights.astype(jnp.bfloat16), raw[:, :LAT], preferred_element_type=jnp.float32
        )
        result = (result * (1.0 / total)).astype(jnp.bfloat16)
        for g in range(GROUP):
            at = (first + g) * 2 * LAT + odd * LAT
            out_ref[:, at : at + LAT] = result[g * BLK : (g + 1) * BLK]

    units = PAIRS // GROUP * 2
    scores = score(0)
    for unit in range(units):
        following = score(unit + 1) if unit + 1 < units else None
        finish(unit, scores)
        scores = following


def body(
    queries,
    prefix_latent,
    window_latent,
    index_queries,
    index_weights,
    prefix_index_keys,
    window_index_keys,
    picks,
):
    devices = lax.axis_size("ctx")
    own = lax.axis_index("ctx").astype(jnp.int32).reshape(1)
    tok = queries.shape[0]
    per_device = tok // BLK
    span = BLK + tok

    def swap(array, rel):
        return lax.ppermute(array, "ctx", [(i, i ^ rel) for i in range(devices)])

    smem = pl.BlockSpec(memory_space=pltpu.SMEM)
    vmem = pl.BlockSpec(memory_space=pltpu.VMEM)
    hbm = pl.BlockSpec(memory_space=pltpu.HBM)
    params = pltpu.CompilerParams(vmem_limit_bytes=VMEM)

    def index_cost(keys):
        return pl.CostEstimate(
            flops=2 * tok * IH * IDX * keys * 4, bytes_accessed=2**22, transcendentals=0
        )

    order_scratch = [pltpu.VMEM((devices * BLK, IDX), jnp.bfloat16)]

    def index_window(shard_keys):
        count = shard_keys.shape[0] // span
        return pl.pallas_call(
            functools.partial(index_window_kernel, count),
            out_shape=jax.ShapeDtypeStruct((count, tok, LANES), jnp.float32),
            in_specs=[vmem, vmem, vmem],
            out_specs=vmem,
            compiler_params=params,
            cost_estimate=index_cost(count * tok),
        )(index_queries, weights, shard_keys)

    def after(done, *arrays):
        return lax.optimization_barrier((done, *arrays))[1:]

    bits = []
    bit = devices // 2
    while bit >= 4:
        bits.append(bit)
        bit //= 2

    low, high = bits[-1], bits[:-1]
    rows = jnp.concatenate([prefix_latent, window_latent], 0).reshape(3 * BLK, ROW)
    rows = jnp.pad(rows, ((0, 0), (0, WIDE - ROW)))
    shards = {0: rows}
    line, key_line = [0], jnp.concatenate([prefix_index_keys, window_index_keys], 0)
    (key_line,) = lax.optimization_barrier((key_line,))
    for bit in bits:
        other = swap(key_line, bit)
        if bit != low:
            (other, held) = lax.optimization_barrier((other, rows))
            shards[bit] = swap(held, bit)
        key_line = jnp.concatenate([key_line, other], 0)
        line = line + [rel ^ bit for rel in line]
        if bit != low:
            touch_on = key_line
    (early_queries, early_weights) = after(touch_on, index_queries, index_weights.T)
    weights = pl.pallas_call(
        weights_kernel,
        out_shape=jax.ShapeDtypeStruct((tok, IH), jnp.float32),
        in_specs=[vmem, vmem],
        out_specs=vmem,
        compiler_params=params,
    )(early_queries, early_weights)
    (held,) = after(key_line, rows)
    for bit in (low, 2):
        shards[bit] = swap(held, bit)
    key_side = swap(key_line, 2)
    side = [rel ^ 2 for rel in line]
    key_far = swap(jnp.concatenate([key_line, key_side], 0), 1)
    far = [rel ^ 1 for rel in line + side]

    def send(done, *moves):
        sources = sorted({rel for rel, _ in moves})
        held = dict(zip(sources, after(done, *[shards[rel] for rel in sources])))
        for rel, bit in moves:
            shards[rel ^ bit] = swap(held[rel], bit)

    line_done = index_window(key_line)
    send(line_done, (0, 1))
    def settle(array, done, rels):
        got = lax.optimization_barrier((array, done, *[shards[rel] for rel in rels]))
        shards.update(zip(rels, got[2:]))
        return got[0]

    side_done = index_window(key_side)
    side_done = settle(side_done, weights, [1, 2])
    send(side_done, *[(bit, 2) for bit in high], (low, 2), (2, 1))
    rest = []
    for n, bit in enumerate(high):
        for other in bits[n + 1 :]:
            for rel in [r for r in [bit] + rest if not r & (2 * other - 1) and r & -r > other]:
                (held,) = after(side_done, shards[rel])
                shards[rel ^ other] = swap(held, other)
                rest.append(rel ^ other)
    far_done = index_window(key_far)
    far_done = settle(far_done, weights, [bit | 2 for bit in high])
    send(
        far_done,
        *[(rel, 2) for rel in rest],
        *[(bit | 2, 1) for bit in high],
        *[(rel, 1) for rel in rest],
        *[(bit, 1) for bit in high],
    )
    held = settle(index_queries, far_done, rest + [3])
    places = [line, side, far]
    tiles = devices * BLK // TILE
    begun = pl.pallas_call(
        functools.partial(index_prefix_kernel, places, 0, tiles // 2),
        out_shape=jax.ShapeDtypeStruct((tok, tiles // 2 * TILE), jnp.float32),
        in_specs=[smem] + [vmem] * 5,
        out_specs=vmem,
        scratch_shapes=order_scratch,
        compiler_params=params,
        cost_estimate=index_cost(tiles // 2 * TILE),
    )(own, held, weights, key_line, key_side, key_far)
    early = [0, 1, 2, 3, low, low | 2] + [rel for bit in high for rel in (bit, bit | 1, bit | 2, bit | 3)]
    early += [rel | n for rel in rest for n in (0, 1)]
    begun = settle(begun, weights, [rel for rel in early if rel])
    send(begun, (low, 1), (low | 2, 1))
    late = [rel for rel in range(devices) if rel not in early]
    prefix_index, window_index, cache = pl.pallas_call(
        functools.partial(index_last_kernel, places, early, tiles // 2, tiles - tiles // 2),
        out_shape=(
            jax.ShapeDtypeStruct((tok, devices * BLK), jnp.float32),
            jax.ShapeDtypeStruct((tok, devices * tok), jnp.float32),
            jax.ShapeDtypeStruct((len(early) + 2, BLK, WIDE), jnp.bfloat16),
        ),
        in_specs=[smem, smem] + [vmem] * 9 + [hbm] * len(early),
        out_specs=(hbm, hbm, vmem),
        scratch_shapes=order_scratch
        + [
            pltpu.VMEM((tok, devices * BLK), jnp.float32),
            pltpu.VMEM((tok, devices * tok), jnp.float32),
            pltpu.SMEM((devices,), jnp.int32),
            pltpu.SemaphoreType.DMA((len(early) + 4,)),
        ],
        compiler_params=params,
        cost_estimate=index_cost(tiles // 2 * TILE),
    )(
        own,
        picks,
        index_queries,
        weights,
        key_line,
        key_side,
        key_far,
        line_done,
        side_done,
        far_done,
        begun,
        *[shards[rel] for rel in early],
    )
    send(prefix_index, *[(rel | 2, 1) for rel in rest])

    count = picks.shape[1] * BLK
    attention = pl.pallas_call(
        functools.partial(attention_kernel, early, late),
        grid_spec=pltpu.PrefetchScalarGridSpec(
            num_scalar_prefetch=2,
            grid=(per_device, H // 2 // PAIRS),
            in_specs=[pl.BlockSpec((BLK, PAIRS * 2 * ROW), lambda b, h, *_: (b, h))]
            + [vmem]
            + [hbm] * len(late),
            out_specs=pl.BlockSpec((BLK, PAIRS * 2 * LAT), lambda b, h, *_: (b, h)),
            scratch_shapes=[
                pltpu.VMEM((len(late), BLK, WIDE), jnp.bfloat16),
                pltpu.VMEM((count, WIDE), jnp.bfloat16),
                pltpu.VMEM((WIDE, count), jnp.bfloat16),
                pltpu.VMEM((WIDE, count), jnp.bfloat16),
                pltpu.SMEM((devices,), jnp.int32),
                pltpu.SMEM((devices,), jnp.int32),
                pltpu.SemaphoreType.DMA((len(late),)),
            ],
        ),
        out_shape=jax.ShapeDtypeStruct((tok, H * LAT), jnp.bfloat16),
        compiler_params=params,
        cost_estimate=pl.CostEstimate(
            flops=2 * tok * H * count * (WIDE + LAT), bytes_accessed=2**24, transcendentals=0
        ),
    )(own, picks, queries, cache, *[shards[rel] for rel in late])
    return (attention, prefix_index, window_index)


def solution(mesh):
    placed = P(("groups", "ctx"), None)
    return jax.shard_map(
        body,
        mesh=mesh,
        in_specs=(placed,) * 8,
        out_specs=(placed,) * 3,
        check_vma=False,
    )
```

```python
import functools

import jax
import jax.numpy as jnp
from jax import lax
from jax.experimental import pallas as pl
from jax.experimental.pallas import tpu as pltpu
from jax.sharding import PartitionSpec as P

H = 64
LAT = 512
ROPE = 64
ROW = LAT + ROPE
WIDE = 640
IH = 64
IDX = 128
BLK = 64
LANES = 128
TILE = 512
TOK_TILE = 32
HEAD_STEP = 16
PAIRS = 8
GROUP = 8
LOW = -1.0e30
EXP2_SCALE = 192.0**-0.5 * 1.4426950408889634
VMEM = 48 * 2**20


def index_tile(iq_ref, weights, keys):
    keys_t = keys.T
    rows, width = iq_ref.shape[0], keys.shape[0]
    parts = []
    for t0 in range(0, rows, TOK_TILE):
        acc = jnp.zeros((TOK_TILE, width), jnp.float32)
        for j0 in range(0, IH, HEAD_STEP):
            lhs = jnp.concatenate(
                [
                    iq_ref[t0 : t0 + TOK_TILE, j * IDX : (j + 1) * IDX]
                    for j in range(j0, j0 + HEAD_STEP)
                ],
                0,
            )
            prod = jnp.dot(lhs, keys_t, preferred_element_type=jnp.float32)
            for j in range(HEAD_STEP):
                weight = jnp.broadcast_to(
                    weights[t0 : t0 + TOK_TILE, j0 + j : j0 + j + 1], (TOK_TILE, LANES)
                )
                weight = jnp.concatenate([weight] * (width // LANES), 1)
                acc = acc + jnp.maximum(prod[j * TOK_TILE : (j + 1) * TOK_TILE], 0.0) * weight
        parts.append(acc)
    return jnp.concatenate(parts, 0)


def window_keys(keys_ref, tok, each, step):
    span = BLK + tok
    return jnp.concatenate(
        [
            keys_ref[pl.ds(pl.multiple_of((step * each + n) * span + BLK, BLK), tok), :]
            for n in range(each)
        ],
        0,
    )


def weights_kernel(iq_ref, w_ref, out_ref):
    out_ref[...] = w_ref[...].T * IDX**-0.5


def index_tiles(iq_ref, w_ref, steps, load, store):
    weights = w_ref[...]

    @pl.loop(0, steps)
    def _(step):
        store(step, index_tile(iq_ref, weights, load(step)))


def index_window_kernel(shards, iq_ref, w_ref, keys_ref, out_ref):
    tok = iq_ref.shape[0]
    each = TILE // tok

    def store(step, value):
        for n in range(each):
            out_ref[step * each + n] = value[:, n * tok : (n + 1) * tok]

    def load(step):
        return window_keys(keys_ref, tok, each, step)

    index_tiles(iq_ref, w_ref, shards // each, load, store)


def order_prefix(places, own, tok, key_refs, keys_ref):
    for ref, rels in zip(key_refs, places):
        for n, rel in enumerate(rels):
            at = pl.multiple_of((own ^ rel) * BLK, BLK)
            span = BLK + tok
            keys_ref[pl.ds(at, BLK), :] = ref[n * span : n * span + BLK, :]


def index_prefix_kernel(places, first, steps, own_ref, iq_ref, w_ref, *refs):
    count = len(places)
    out_ref, keys_ref = refs[count:]
    order_prefix(places, own_ref[0], iq_ref.shape[0], refs[:count], keys_ref)

    def load(step):
        return keys_ref[pl.ds(pl.multiple_of((first + step) * TILE, TILE), TILE), :]

    def store(step, value):
        out_ref[:, pl.ds(pl.multiple_of(step * TILE, TILE), TILE)] = value

    index_tiles(iq_ref, w_ref, steps, load, store)


def index_last_kernel(places, first, steps, own_ref, iq_ref, w_ref, *refs):
    count = len(places)
    key_refs, done_refs = refs[:count], refs[count : 2 * count]
    begun_ref, prefix_ref, window_ref, keys_ref = refs[2 * count :]
    own = own_ref[0]
    tok = iq_ref.shape[0]
    order_prefix(places, own, tok, key_refs, keys_ref)
    prefix_ref[:, : first * TILE] = begun_ref[...]
    row = lax.broadcasted_iota(jnp.int32, (tok, LANES), 0)
    lane = lax.broadcasted_iota(jnp.int32, (tok, LANES), 1)
    for ref, rels in zip(done_refs, places):
        for n, rel in enumerate(rels):
            other = own ^ rel
            seen = other * tok + lane <= own * tok + row
            window_ref[:, pl.ds(pl.multiple_of(other * tok, LANES), LANES)] = jnp.where(
                seen, ref[n], 0.0
            )

    def load(step):
        return keys_ref[pl.ds(pl.multiple_of((first + step) * TILE, TILE), TILE), :]

    def store(step, value):
        prefix_ref[:, pl.ds(pl.multiple_of((first + step) * TILE, TILE), TILE)] = value

    index_tiles(iq_ref, w_ref, steps, load, store)


def attention_kernel(devices, own_ref, pick_ref, q_ref, *refs):
    shards = refs[:devices]
    out_ref, cache, raw, even_t, odd_t, need = refs[devices:]
    block = pl.program_id(0)
    own = own_ref[0]
    picks = pick_ref.shape[1]

    def split(pick):
        window = pick - devices
        holder = jnp.where(window < 0, pick, window // 2)
        return holder ^ own, jnp.where(window < 0, 0, 1 + window % 2)

    @pl.when((block == 0) & (pl.program_id(1) == 0))
    def _():
        for rel in range(devices):
            need[rel] = 0
        for b in range(pick_ref.shape[0]):
            for s in range(picks):
                rel, inner = split(pick_ref[b, s])
                need[rel] = inner
        for rel in range(1, devices):
            at = pl.multiple_of(need[rel] * BLK, BLK)
            cache[rel] = shards[rel][pl.ds(at, BLK), :]
        for n in range(3):
            cache[0 if n == 0 else devices - 1 + n] = shards[0][n * BLK : (n + 1) * BLK, :]

    @pl.when(pl.program_id(1) == 0)
    def _():
        own_pick = devices + own * 2 + block
        own_slot = jnp.int32(0)
        for s in range(picks):
            own_slot = jnp.where(pick_ref[block, s] == own_pick, s, own_slot)
        for s in range(picks):
            place = jnp.where(own_slot == s, picks - 1, own_slot if s == picks - 1 else s)
            rel, inner = split(pick_ref[block, s])
            slot = jnp.where((rel == 0) & (inner > 0), devices - 1 + inner, rel)
            raw[pl.ds(pl.multiple_of(place * BLK, BLK), BLK), :] = cache[slot]
        turned = raw[...].T
        even_t[...] = turned
        odd_t[0:ROPE] = turned[ROW:WIDE]
        odd_t[ROPE:WIDE] = turned[0:ROW]

    count = picks * BLK
    row = lax.broadcasted_iota(jnp.int32, (BLK, LANES), 0)
    lane = lax.broadcasted_iota(jnp.int32, (BLK, LANES), 1)
    allowed = jnp.concatenate([lane - BLK <= row] * GROUP, 0)

    def score(unit):
        odd, first = unit % 2, unit // 2 * GROUP
        lhs = jnp.concatenate(
            [
                q_ref[:, (first + g) * 2 * ROW + odd * LAT : (first + g) * 2 * ROW + odd * LAT + WIDE]
                for g in range(GROUP)
            ],
            0,
        )
        return jnp.dot(lhs, (odd_t if odd else even_t)[...], preferred_element_type=jnp.float32)

    def finish(unit, scores):
        odd, first = unit % 2, unit // 2 * GROUP
        last = jnp.where(allowed, scores[:, count - LANES :], LOW)
        scores = jnp.concatenate([scores[:, : count - LANES], last], 1)
        peak = jnp.max(scores, axis=1, keepdims=True)
        weights = jnp.exp2((scores - peak) * EXP2_SCALE)
        total = jnp.sum(weights, axis=1, keepdims=True)
        result = jnp.dot(
            weights.astype(jnp.bfloat16), raw[:, :LAT], preferred_element_type=jnp.float32
        )
        result = (result * (1.0 / total)).astype(jnp.bfloat16)
        for g in range(GROUP):
            at = (first + g) * 2 * LAT + odd * LAT
            out_ref[:, at : at + LAT] = result[g * BLK : (g + 1) * BLK]

    units = PAIRS // GROUP * 2
    scores = score(0)
    for unit in range(units):
        following = score(unit + 1) if unit + 1 < units else None
        finish(unit, scores)
        scores = following


def body(
    queries,
    prefix_latent,
    window_latent,
    index_queries,
    index_weights,
    prefix_index_keys,
    window_index_keys,
    picks,
):
    devices = lax.axis_size("ctx")
    own = lax.axis_index("ctx").astype(jnp.int32).reshape(1)
    tok = queries.shape[0]
    per_device = tok // BLK
    span = BLK + tok

    def swap(array, rel):
        return lax.ppermute(array, "ctx", [(i, i ^ rel) for i in range(devices)])

    smem = pl.BlockSpec(memory_space=pltpu.SMEM)
    vmem = pl.BlockSpec(memory_space=pltpu.VMEM)
    params = pltpu.CompilerParams(vmem_limit_bytes=VMEM)

    def index_cost(keys):
        return pl.CostEstimate(
            flops=2 * tok * IH * IDX * keys * 4, bytes_accessed=2**22, transcendentals=0
        )

    order_scratch = [pltpu.VMEM((devices * BLK, IDX), jnp.bfloat16)]

    def index_window(shard_keys):
        count = shard_keys.shape[0] // span
        return pl.pallas_call(
            functools.partial(index_window_kernel, count),
            out_shape=jax.ShapeDtypeStruct((count, tok, LANES), jnp.float32),
            in_specs=[vmem, vmem, vmem],
            out_specs=vmem,
            compiler_params=params,
            cost_estimate=index_cost(count * tok),
        )(index_queries, weights, shard_keys)

    def after(done, *arrays):
        return lax.optimization_barrier((done, *arrays))[1:]

    bits = []
    bit = devices // 2
    while bit >= 4:
        bits.append(bit)
        bit //= 2

    low, high = bits[-1], bits[:-1]
    rows = jnp.concatenate([prefix_latent, window_latent], 0).reshape(3 * BLK, ROW)
    rows = jnp.pad(rows, ((0, 0), (0, WIDE - ROW)))
    shards = {0: rows}
    line, key_line = [0], jnp.concatenate([prefix_index_keys, window_index_keys], 0)
    (key_line,) = lax.optimization_barrier((key_line,))
    (early_queries, early_weights) = after(rows, index_queries, index_weights.T)
    weights = pl.pallas_call(
        weights_kernel,
        out_shape=jax.ShapeDtypeStruct((tok, IH), jnp.float32),
        in_specs=[vmem, vmem],
        out_specs=vmem,
        compiler_params=params,
    )(early_queries, early_weights)
    for bit in bits:
        other = swap(key_line, bit)
        if bit != low:
            (other, held, weights) = lax.optimization_barrier((other, rows, weights))
            shards[bit] = swap(held, bit)
        key_line = jnp.concatenate([key_line, other], 0)
        line = line + [rel ^ bit for rel in line]
    (held,) = after(key_line, rows)
    for bit in (low, 2):
        shards[bit] = swap(held, bit)
    key_side = swap(key_line, 2)
    side = [rel ^ 2 for rel in line]
    key_far = swap(jnp.concatenate([key_line, key_side], 0), 1)
    far = [rel ^ 1 for rel in line + side]

    def send(done, *moves):
        sources = sorted({rel for rel, _ in moves})
        held = dict(zip(sources, after(done, *[shards[rel] for rel in sources])))
        for rel, bit in moves:
            shards[rel ^ bit] = swap(held[rel], bit)

    line_done = index_window(key_line)
    send(line_done, (0, 1))
    def settle(array, done, rels):
        got = lax.optimization_barrier((array, done, *[shards[rel] for rel in rels]))
        shards.update(zip(rels, got[2:]))
        return got[0]

    side_done = index_window(key_side)
    side_done = settle(side_done, weights, [1, 2])
    send(side_done, *[(bit, 2) for bit in high], (low, 2), (2, 1))
    rest = []
    for n, bit in enumerate(high):
        for other in bits[n + 1 :]:
            for rel in [r for r in [bit] + rest if not r & (2 * other - 1) and r & -r > other]:
                (held,) = after(side_done, shards[rel])
                shards[rel ^ other] = swap(held, other)
                rest.append(rel ^ other)
    far_done = index_window(key_far)
    send(far_done, *[(rel, 2) for rel in rest], *[(rel, 1) for rel in bits])
    held = settle(index_queries, far_done, rest + [3])
    places = [line, side, far]
    tiles = devices * BLK // TILE
    begun = pl.pallas_call(
        functools.partial(index_prefix_kernel, places, 0, tiles // 2),
        out_shape=jax.ShapeDtypeStruct((tok, tiles // 2 * TILE), jnp.float32),
        in_specs=[smem] + [vmem] * 5,
        out_specs=vmem,
        scratch_shapes=order_scratch,
        compiler_params=params,
        cost_estimate=index_cost(tiles // 2 * TILE),
    )(own, held, weights, key_line, key_side, key_far)
    send(begun, *[(bit | 2, 1) for bit in bits], *[(rel, 1) for rel in rest])
    held = settle(index_queries, begun, [rel ^ 1 for rel in bits] + [rel | 2 for rel in bits])
    prefix_index, window_index = pl.pallas_call(
        functools.partial(index_last_kernel, places, tiles // 2, tiles - tiles // 2),
        out_shape=(
            jax.ShapeDtypeStruct((tok, devices * BLK), jnp.float32),
            jax.ShapeDtypeStruct((tok, devices * tok), jnp.float32),
        ),
        in_specs=[smem] + [vmem] * 9,
        out_specs=(vmem, vmem),
        scratch_shapes=order_scratch,
        compiler_params=params,
        cost_estimate=index_cost(tiles // 2 * TILE),
    )(
        own,
        held,
        weights,
        key_line,
        key_side,
        key_far,
        line_done,
        side_done,
        far_done,
        begun,
    )
    send(prefix_index, *[(rel | 2, 1) for rel in rest])
    shards = [shards[rel] for rel in range(devices)]

    count = picks.shape[1] * BLK
    attention = pl.pallas_call(
        functools.partial(attention_kernel, devices),
        grid_spec=pltpu.PrefetchScalarGridSpec(
            num_scalar_prefetch=2,
            grid=(per_device, H // 2 // PAIRS),
            in_specs=[pl.BlockSpec((BLK, PAIRS * 2 * ROW), lambda b, h, *_: (b, h))]
            + [vmem] * devices,
            out_specs=pl.BlockSpec((BLK, PAIRS * 2 * LAT), lambda b, h, *_: (b, h)),
            scratch_shapes=[
                pltpu.VMEM((devices + 2, BLK, WIDE), jnp.bfloat16),
                pltpu.VMEM((count, WIDE), jnp.bfloat16),
                pltpu.VMEM((WIDE, count), jnp.bfloat16),
                pltpu.VMEM((WIDE, count), jnp.bfloat16),
                pltpu.SMEM((devices,), jnp.int32),
            ],
        ),
        out_shape=jax.ShapeDtypeStruct((tok, H * LAT), jnp.bfloat16),
        compiler_params=params,
        cost_estimate=pl.CostEstimate(
            flops=2 * tok * H * count * (WIDE + LAT), bytes_accessed=2**24, transcendentals=0
        ),
    )(own, picks, queries, *shards)
    return (attention, prefix_index, window_index)


def solution(mesh):
    placed = P(("groups", "ctx"), None)
    return jax.shard_map(
        body,
        mesh=mesh,
        in_specs=(placed,) * 8,
        out_specs=(placed,) * 3,
        check_vma=False,
    )
```

```python
import functools

import jax
import jax.numpy as jnp
from jax import lax
from jax.experimental import pallas as pl
from jax.experimental.pallas import tpu as pltpu
from jax.sharding import PartitionSpec as P

H = 64
LAT = 512
ROPE = 64
ROW = LAT + ROPE
WIDE = 640
IH = 64
IDX = 128
BLK = 64
LANES = 128
TILE = 512
TOK_TILE = 32
HEAD_STEP = 16
PAIRS = 8
GROUP = 8
LOW = -1.0e30
EXP2_SCALE = 192.0**-0.5 * 1.4426950408889634
VMEM = 48 * 2**20
COPY_VMEM = 50 * 2**20


def index_tile(iq_ref, weights, keys):
    keys_t = keys.T
    rows, width = iq_ref.shape[0], keys.shape[0]
    parts = []
    for t0 in range(0, rows, TOK_TILE):
        acc = jnp.zeros((TOK_TILE, width), jnp.float32)
        for j0 in range(0, IH, HEAD_STEP):
            lhs = jnp.concatenate(
                [
                    iq_ref[t0 : t0 + TOK_TILE, j * IDX : (j + 1) * IDX]
                    for j in range(j0, j0 + HEAD_STEP)
                ],
                0,
            )
            prod = jnp.dot(lhs, keys_t, preferred_element_type=jnp.float32)
            for j in range(HEAD_STEP):
                weight = jnp.broadcast_to(
                    weights[t0 : t0 + TOK_TILE, j0 + j : j0 + j + 1], (TOK_TILE, LANES)
                )
                weight = jnp.concatenate([weight] * (width // LANES), 1)
                acc = acc + jnp.maximum(prod[j * TOK_TILE : (j + 1) * TOK_TILE], 0.0) * weight
        parts.append(acc)
    return jnp.concatenate(parts, 0)


def window_keys(keys_ref, tok, each, step):
    span = BLK + tok
    return jnp.concatenate(
        [
            keys_ref[pl.ds(pl.multiple_of((step * each + n) * span + BLK, BLK), tok), :]
            for n in range(each)
        ],
        0,
    )


def weights_kernel(iq_hbm, w_hbm, iq_ref, out_ref, w_ref, sem):
    copies = [
        pltpu.make_async_copy(iq_hbm, iq_ref, sem.at[0]),
        pltpu.make_async_copy(w_hbm, w_ref, sem.at[1]),
    ]
    for copy in copies:
        copy.start()
    for copy in copies[::-1]:
        copy.wait()
    out_ref[...] = w_ref[...].T * IDX**-0.5


def index_tiles(iq_ref, w_ref, steps, load, store):
    weights = w_ref[...]

    @pl.loop(0, steps)
    def _(step):
        store(step, index_tile(iq_ref, weights, load(step)))


def index_window_kernel(shards, iq_ref, w_ref, keys_ref, out_ref):
    tok = iq_ref.shape[0]
    each = TILE // tok

    def store(step, value):
        for n in range(each):
            out_ref[step * each + n] = value[:, n * tok : (n + 1) * tok]

    def load(step):
        return window_keys(keys_ref, tok, each, step)

    index_tiles(iq_ref, w_ref, shards // each, load, store)


def order_prefix(places, own, tok, key_refs, keys_ref):
    for ref, rels in zip(key_refs, places):
        for n, rel in enumerate(rels):
            at = pl.multiple_of((own ^ rel) * BLK, BLK)
            span = BLK + tok
            keys_ref[pl.ds(at, BLK), :] = ref[n * span : n * span + BLK, :]


def index_prefix_kernel(places, first, steps, own_ref, iq_ref, w_ref, *refs):
    count = len(places)
    out_ref, keys_ref = refs[count:]
    order_prefix(places, own_ref[0], iq_ref.shape[0], refs[:count], keys_ref)

    def load(step):
        return keys_ref[pl.ds(pl.multiple_of((first + step) * TILE, TILE), TILE), :]

    def store(step, value):
        out_ref[:, pl.ds(pl.multiple_of(step * TILE, TILE), TILE)] = value

    index_tiles(iq_ref, w_ref, steps, load, store)


def index_last_kernel(places, first, steps, own_ref, iq_ref, w_ref, *refs):
    count = len(places)
    key_refs, done_refs = refs[:count], refs[count : 2 * count]
    begun_ref, prefix_ref, window_ref, keys_ref = refs[2 * count :]
    own = own_ref[0]
    tok = iq_ref.shape[0]
    order_prefix(places, own, tok, key_refs, keys_ref)
    prefix_ref[:, : first * TILE] = begun_ref[...]
    row = lax.broadcasted_iota(jnp.int32, (tok, LANES), 0)
    lane = lax.broadcasted_iota(jnp.int32, (tok, LANES), 1)
    for ref, rels in zip(done_refs, places):
        for n, rel in enumerate(rels):
            other = own ^ rel
            seen = other * tok + lane <= own * tok + row
            window_ref[:, pl.ds(pl.multiple_of(other * tok, LANES), LANES)] = jnp.where(
                seen, ref[n], 0.0
            )

    def load(step):
        return keys_ref[pl.ds(pl.multiple_of((first + step) * TILE, TILE), TILE), :]

    def store(step, value):
        prefix_ref[:, pl.ds(pl.multiple_of((first + step) * TILE, TILE), TILE)] = value

    index_tiles(iq_ref, w_ref, steps, load, store)


def attention_kernel(devices, own_ref, pick_ref, q_ref, *refs):
    shards = refs[:devices]
    out_ref, cache, raw, even_t, odd_t, need = refs[devices:]
    block = pl.program_id(0)
    own = own_ref[0]
    picks = pick_ref.shape[1]

    def split(pick):
        window = pick - devices
        holder = jnp.where(window < 0, pick, window // 2)
        return holder ^ own, jnp.where(window < 0, 0, 1 + window % 2)

    @pl.when((block == 0) & (pl.program_id(1) == 0))
    def _():
        for rel in range(devices):
            need[rel] = 0
        for b in range(pick_ref.shape[0]):
            for s in range(picks):
                rel, inner = split(pick_ref[b, s])
                need[rel] = inner
        for rel in range(1, devices):
            at = pl.multiple_of(need[rel] * BLK, BLK)
            cache[rel] = shards[rel][pl.ds(at, BLK), :]
        for n in range(3):
            cache[0 if n == 0 else devices - 1 + n] = shards[0][n * BLK : (n + 1) * BLK, :]

    @pl.when(pl.program_id(1) == 0)
    def _():
        own_pick = devices + own * 2 + block
        own_slot = jnp.int32(0)
        for s in range(picks):
            own_slot = jnp.where(pick_ref[block, s] == own_pick, s, own_slot)
        for s in range(picks):
            place = jnp.where(own_slot == s, picks - 1, own_slot if s == picks - 1 else s)
            rel, inner = split(pick_ref[block, s])
            slot = jnp.where((rel == 0) & (inner > 0), devices - 1 + inner, rel)
            raw[pl.ds(pl.multiple_of(place * BLK, BLK), BLK), :] = cache[slot]
        turned = raw[...].T
        even_t[...] = turned
        odd_t[0:ROPE] = turned[ROW:WIDE]
        odd_t[ROPE:WIDE] = turned[0:ROW]

    count = picks * BLK
    row = lax.broadcasted_iota(jnp.int32, (BLK, LANES), 0)
    lane = lax.broadcasted_iota(jnp.int32, (BLK, LANES), 1)
    allowed = jnp.concatenate([lane - BLK <= row] * GROUP, 0)

    def score(unit):
        odd, first = unit % 2, unit // 2 * GROUP
        lhs = jnp.concatenate(
            [
                q_ref[:, (first + g) * 2 * ROW + odd * LAT : (first + g) * 2 * ROW + odd * LAT + WIDE]
                for g in range(GROUP)
            ],
            0,
        )
        return jnp.dot(lhs, (odd_t if odd else even_t)[...], preferred_element_type=jnp.float32)

    def finish(unit, scores):
        odd, first = unit % 2, unit // 2 * GROUP
        last = jnp.where(allowed, scores[:, count - LANES :], LOW)
        scores = jnp.concatenate([scores[:, : count - LANES], last], 1)
        peak = jnp.max(scores, axis=1, keepdims=True)
        weights = jnp.exp2((scores - peak) * EXP2_SCALE)
        total = jnp.sum(weights, axis=1, keepdims=True)
        result = jnp.dot(
            weights.astype(jnp.bfloat16), raw[:, :LAT], preferred_element_type=jnp.float32
        )
        result = (result * (1.0 / total)).astype(jnp.bfloat16)
        for g in range(GROUP):
            at = (first + g) * 2 * LAT + odd * LAT
            out_ref[:, at : at + LAT] = result[g * BLK : (g + 1) * BLK]

    units = PAIRS // GROUP * 2
    scores = score(0)
    for unit in range(units):
        following = score(unit + 1) if unit + 1 < units else None
        finish(unit, scores)
        scores = following


def body(
    queries,
    prefix_latent,
    window_latent,
    index_queries,
    index_weights,
    prefix_index_keys,
    window_index_keys,
    picks,
):
    devices = lax.axis_size("ctx")
    own = lax.axis_index("ctx").astype(jnp.int32).reshape(1)
    tok = queries.shape[0]
    per_device = tok // BLK
    span = BLK + tok

    def swap(array, rel):
        return lax.ppermute(array, "ctx", [(i, i ^ rel) for i in range(devices)])

    smem = pl.BlockSpec(memory_space=pltpu.SMEM)
    vmem = pl.BlockSpec(memory_space=pltpu.VMEM)
    params = pltpu.CompilerParams(vmem_limit_bytes=VMEM)

    def index_cost(keys):
        return pl.CostEstimate(
            flops=2 * tok * IH * IDX * keys * 4, bytes_accessed=2**22, transcendentals=0
        )

    order_scratch = [pltpu.VMEM((devices * BLK, IDX), jnp.bfloat16)]

    def index_window(shard_keys):
        count = shard_keys.shape[0] // span
        return pl.pallas_call(
            functools.partial(index_window_kernel, count),
            out_shape=jax.ShapeDtypeStruct((count, tok, LANES), jnp.float32),
            in_specs=[vmem, vmem, vmem],
            out_specs=vmem,
            compiler_params=params,
            cost_estimate=index_cost(count * tok),
        )(index_queries, weights, shard_keys)

    def after(done, *arrays):
        return lax.optimization_barrier((done, *arrays))[1:]

    bits = []
    bit = devices // 2
    while bit >= 4:
        bits.append(bit)
        bit //= 2

    low, high = bits[-1], bits[:-1]
    rows = jnp.concatenate([prefix_latent, window_latent], 0).reshape(3 * BLK, ROW)
    rows = jnp.pad(rows, ((0, 0), (0, WIDE - ROW)))
    shards = {0: rows}
    line, key_line = [0], jnp.concatenate([prefix_index_keys, window_index_keys], 0)
    (key_line,) = lax.optimization_barrier((key_line,))
    (early_queries, early_weights) = after(rows, index_queries, index_weights.T)
    index_queries, weights = pl.pallas_call(
        weights_kernel,
        out_shape=(
            jax.ShapeDtypeStruct(index_queries.shape, index_queries.dtype),
            jax.ShapeDtypeStruct((tok, IH), jnp.float32),
        ),
        in_specs=[pl.BlockSpec(memory_space=pl.ANY)] * 2,
        out_specs=(vmem, vmem),
        scratch_shapes=[pltpu.VMEM((IH, tok), jnp.float32), pltpu.SemaphoreType.DMA((2,))],
        compiler_params=pltpu.CompilerParams(vmem_limit_bytes=COPY_VMEM),
    )(early_queries, early_weights)
    for bit in bits:
        other = swap(key_line, bit)
        if bit != low:
            (other, held, weights) = lax.optimization_barrier((other, rows, weights))
            shards[bit] = swap(held, bit)
        key_line = jnp.concatenate([key_line, other], 0)
        line = line + [rel ^ bit for rel in line]
    (held,) = after(key_line, rows)
    for bit in (low, 2):
        shards[bit] = swap(held, bit)
    key_side = swap(key_line, 2)
    side = [rel ^ 2 for rel in line]
    key_far = swap(jnp.concatenate([key_line, key_side], 0), 1)
    far = [rel ^ 1 for rel in line + side]

    def send(done, *moves):
        sources = sorted({rel for rel, _ in moves})
        held = dict(zip(sources, after(done, *[shards[rel] for rel in sources])))
        for rel, bit in moves:
            shards[rel ^ bit] = swap(held[rel], bit)

    line_done = index_window(key_line)
    send(line_done, (0, 1))
    def settle(array, done, rels):
        got = lax.optimization_barrier((array, done, *[shards[rel] for rel in rels]))
        shards.update(zip(rels, got[2:]))
        return got[0]

    side_done = index_window(key_side)
    side_done = settle(side_done, weights, [1, 2])
    send(side_done, *[(bit, 2) for bit in high], (low, 2), (2, 1))
    rest = []
    for n, bit in enumerate(high):
        for other in bits[n + 1 :]:
            for rel in [r for r in [bit] + rest if not r & (2 * other - 1) and r & -r > other]:
                (held,) = after(side_done, shards[rel])
                shards[rel ^ other] = swap(held, other)
                rest.append(rel ^ other)
    far_done = index_window(key_far)
    send(far_done, *[(rel, 2) for rel in rest], *[(rel, 1) for rel in bits])
    held = settle(index_queries, far_done, rest + [3])
    places = [line, side, far]
    tiles = devices * BLK // TILE
    begun = pl.pallas_call(
        functools.partial(index_prefix_kernel, places, 0, tiles // 2),
        out_shape=jax.ShapeDtypeStruct((tok, tiles // 2 * TILE), jnp.float32),
        in_specs=[smem] + [vmem] * 5,
        out_specs=vmem,
        scratch_shapes=order_scratch,
        compiler_params=params,
        cost_estimate=index_cost(tiles // 2 * TILE),
    )(own, held, weights, key_line, key_side, key_far)
    send(begun, *[(bit | 2, 1) for bit in high], *[(rel, 1) for rel in rest])
    held = settle(index_queries, begun, [rel ^ 1 for rel in bits] + [rel | 2 for rel in high])
    prefix_index, window_index = pl.pallas_call(
        functools.partial(index_last_kernel, places, tiles // 2, tiles - tiles // 2),
        out_shape=(
            jax.ShapeDtypeStruct((tok, devices * BLK), jnp.float32),
            jax.ShapeDtypeStruct((tok, devices * tok), jnp.float32),
        ),
        in_specs=[smem] + [vmem] * 9,
        out_specs=(vmem, vmem),
        scratch_shapes=order_scratch,
        compiler_params=params,
        cost_estimate=index_cost(tiles // 2 * TILE),
    )(
        own,
        held,
        weights,
        key_line,
        key_side,
        key_far,
        line_done,
        side_done,
        far_done,
        begun,
    )
    send(prefix_index, (low | 2, 1), *[(rel | 2, 1) for rel in rest])
    shards = [shards[rel] for rel in range(devices)]

    count = picks.shape[1] * BLK
    attention = pl.pallas_call(
        functools.partial(attention_kernel, devices),
        grid_spec=pltpu.PrefetchScalarGridSpec(
            num_scalar_prefetch=2,
            grid=(per_device, H // 2 // PAIRS),
            in_specs=[pl.BlockSpec((BLK, PAIRS * 2 * ROW), lambda b, h, *_: (b, h))]
            + [vmem] * devices,
            out_specs=pl.BlockSpec((BLK, PAIRS * 2 * LAT), lambda b, h, *_: (b, h)),
            scratch_shapes=[
                pltpu.VMEM((devices + 2, BLK, WIDE), jnp.bfloat16),
                pltpu.VMEM((count, WIDE), jnp.bfloat16),
                pltpu.VMEM((WIDE, count), jnp.bfloat16),
                pltpu.VMEM((WIDE, count), jnp.bfloat16),
                pltpu.SMEM((devices,), jnp.int32),
            ],
        ),
        out_shape=jax.ShapeDtypeStruct((tok, H * LAT), jnp.bfloat16),
        compiler_params=params,
        cost_estimate=pl.CostEstimate(
            flops=2 * tok * H * count * (WIDE + LAT), bytes_accessed=2**24, transcendentals=0
        ),
    )(own, picks, queries, *shards)
    return (attention, prefix_index, window_index)


def solution(mesh):
    placed = P(("groups", "ctx"), None)
    return jax.shard_map(
        body,
        mesh=mesh,
        in_specs=(placed,) * 8,
        out_specs=(placed,) * 3,
        check_vma=False,
    )
```

```python
import functools

import jax
import jax.numpy as jnp
from jax import lax
from jax.experimental import pallas as pl
from jax.experimental.pallas import tpu as pltpu
from jax.sharding import PartitionSpec as P

H = 64
LAT = 512
ROPE = 64
ROW = LAT + ROPE
WIDE = 640
IH = 64
IDX = 128
BLK = 64
LANES = 128
TILE = 512
TOK_TILE = 32
HEAD_STEP = 16
PAIRS = 8
GROUP = 8
LOW = -1.0e30
EXP2_SCALE = 192.0**-0.5 * 1.4426950408889634
VMEM = 48 * 2**20
COPY_VMEM = 50 * 2**20


def index_tile(iq_ref, weights, keys):
    keys_t = keys.T
    rows, width = iq_ref.shape[0], keys.shape[0]
    parts = []
    for t0 in range(0, rows, TOK_TILE):
        acc = jnp.zeros((TOK_TILE, width), jnp.float32)
        for j0 in range(0, IH, HEAD_STEP):
            lhs = jnp.concatenate(
                [
                    iq_ref[t0 : t0 + TOK_TILE, j * IDX : (j + 1) * IDX]
                    for j in range(j0, j0 + HEAD_STEP)
                ],
                0,
            )
            prod = jnp.dot(lhs, keys_t, preferred_element_type=jnp.float32)
            for j in range(HEAD_STEP):
                weight = jnp.broadcast_to(
                    weights[t0 : t0 + TOK_TILE, j0 + j : j0 + j + 1], (TOK_TILE, LANES)
                )
                weight = jnp.concatenate([weight] * (width // LANES), 1)
                acc = acc + jnp.maximum(prod[j * TOK_TILE : (j + 1) * TOK_TILE], 0.0) * weight
        parts.append(acc)
    return jnp.concatenate(parts, 0)


def window_keys(keys_ref, tok, each, step):
    span = BLK + tok
    return jnp.concatenate(
        [
            keys_ref[pl.ds(pl.multiple_of((step * each + n) * span + BLK, BLK), tok), :]
            for n in range(each)
        ],
        0,
    )


def weights_kernel(iq_hbm, w_hbm, iq_ref, out_ref, w_ref, sem):
    copies = [
        pltpu.make_async_copy(iq_hbm, iq_ref, sem.at[0]),
        pltpu.make_async_copy(w_hbm, w_ref, sem.at[1]),
    ]
    for copy in copies:
        copy.start()
    for copy in copies[::-1]:
        copy.wait()
    out_ref[...] = w_ref[...].T * IDX**-0.5


def index_tiles(iq_ref, w_ref, steps, load, store):
    weights = w_ref[...]

    @pl.loop(0, steps)
    def _(step):
        store(step, index_tile(iq_ref, weights, load(step)))


def index_window_kernel(shards, iq_ref, w_ref, keys_ref, out_ref):
    tok = iq_ref.shape[0]
    each = TILE // tok

    def store(step, value):
        for n in range(each):
            out_ref[step * each + n] = value[:, n * tok : (n + 1) * tok]

    def load(step):
        return window_keys(keys_ref, tok, each, step)

    index_tiles(iq_ref, w_ref, shards // each, load, store)


def order_prefix(places, own, tok, key_refs, keys_ref):
    for ref, rels in zip(key_refs, places):
        for n, rel in enumerate(rels):
            at = pl.multiple_of((own ^ rel) * BLK, BLK)
            span = BLK + tok
            keys_ref[pl.ds(at, BLK), :] = ref[n * span : n * span + BLK, :]


def index_prefix_kernel(places, first, steps, own_ref, iq_ref, w_ref, *refs):
    count = len(places)
    out_ref, keys_ref = refs[count:]
    order_prefix(places, own_ref[0], iq_ref.shape[0], refs[:count], keys_ref)

    def load(step):
        return keys_ref[pl.ds(pl.multiple_of((first + step) * TILE, TILE), TILE), :]

    def store(step, value):
        out_ref[:, pl.ds(pl.multiple_of(step * TILE, TILE), TILE)] = value

    index_tiles(iq_ref, w_ref, steps, load, store)


def index_last_kernel(places, first, steps, own_ref, iq_ref, w_ref, *refs):
    count = len(places)
    key_refs, done_refs = refs[:count], refs[count : 2 * count]
    begun_ref, prefix_ref, window_ref, keys_ref = refs[2 * count :]
    own = own_ref[0]
    tok = iq_ref.shape[0]
    order_prefix(places, own, tok, key_refs, keys_ref)
    prefix_ref[:, : first * TILE] = begun_ref[...]
    row = lax.broadcasted_iota(jnp.int32, (tok, LANES), 0)
    lane = lax.broadcasted_iota(jnp.int32, (tok, LANES), 1)
    for ref, rels in zip(done_refs, places):
        for n, rel in enumerate(rels):
            other = own ^ rel
            seen = other * tok + lane <= own * tok + row
            window_ref[:, pl.ds(pl.multiple_of(other * tok, LANES), LANES)] = jnp.where(
                seen, ref[n], 0.0
            )

    def load(step):
        return keys_ref[pl.ds(pl.multiple_of((first + step) * TILE, TILE), TILE), :]

    def store(step, value):
        prefix_ref[:, pl.ds(pl.multiple_of((first + step) * TILE, TILE), TILE)] = value

    index_tiles(iq_ref, w_ref, steps, load, store)


def attention_kernel(devices, own_ref, pick_ref, q_ref, *refs):
    shards = refs[:devices]
    out_ref, cache, raw, even_t, odd_t, need = refs[devices:]
    block = pl.program_id(0)
    own = own_ref[0]
    picks = pick_ref.shape[1]

    def split(pick):
        window = pick - devices
        holder = jnp.where(window < 0, pick, window // 2)
        return holder ^ own, jnp.where(window < 0, 0, 1 + window % 2)

    @pl.when((block == 0) & (pl.program_id(1) == 0))
    def _():
        for rel in range(devices):
            need[rel] = 0
        for b in range(pick_ref.shape[0]):
            for s in range(picks):
                rel, inner = split(pick_ref[b, s])
                need[rel] = inner
        for rel in range(1, devices):
            at = pl.multiple_of(need[rel] * BLK, BLK)
            cache[rel] = shards[rel][pl.ds(at, BLK), :]
        for n in range(3):
            cache[0 if n == 0 else devices - 1 + n] = shards[0][n * BLK : (n + 1) * BLK, :]

    @pl.when(pl.program_id(1) == 0)
    def _():
        own_pick = devices + own * 2 + block
        own_slot = jnp.int32(0)
        for s in range(picks):
            own_slot = jnp.where(pick_ref[block, s] == own_pick, s, own_slot)
        for s in range(picks):
            place = jnp.where(own_slot == s, picks - 1, own_slot if s == picks - 1 else s)
            rel, inner = split(pick_ref[block, s])
            slot = jnp.where((rel == 0) & (inner > 0), devices - 1 + inner, rel)
            raw[pl.ds(pl.multiple_of(place * BLK, BLK), BLK), :] = cache[slot]
        turned = raw[...].T
        even_t[...] = turned
        odd_t[0:ROPE] = turned[ROW:WIDE]
        odd_t[ROPE:WIDE] = turned[0:ROW]

    count = picks * BLK
    row = lax.broadcasted_iota(jnp.int32, (BLK, LANES), 0)
    lane = lax.broadcasted_iota(jnp.int32, (BLK, LANES), 1)
    allowed = jnp.concatenate([lane - BLK <= row] * GROUP, 0)

    def score(unit):
        odd, first = unit % 2, unit // 2 * GROUP
        lhs = jnp.concatenate(
            [
                q_ref[:, (first + g) * 2 * ROW + odd * LAT : (first + g) * 2 * ROW + odd * LAT + WIDE]
                for g in range(GROUP)
            ],
            0,
        )
        return jnp.dot(lhs, (odd_t if odd else even_t)[...], preferred_element_type=jnp.float32)

    def finish(unit, scores):
        odd, first = unit % 2, unit // 2 * GROUP
        last = jnp.where(allowed, scores[:, count - LANES :], LOW)
        scores = jnp.concatenate([scores[:, : count - LANES], last], 1)
        peak = jnp.max(scores, axis=1, keepdims=True)
        weights = jnp.exp2((scores - peak) * EXP2_SCALE)
        total = jnp.sum(weights, axis=1, keepdims=True)
        result = jnp.dot(
            weights.astype(jnp.bfloat16), raw[:, :LAT], preferred_element_type=jnp.float32
        )
        result = (result * (1.0 / total)).astype(jnp.bfloat16)
        for g in range(GROUP):
            at = (first + g) * 2 * LAT + odd * LAT
            out_ref[:, at : at + LAT] = result[g * BLK : (g + 1) * BLK]

    units = PAIRS // GROUP * 2
    scores = score(0)
    for unit in range(units):
        following = score(unit + 1) if unit + 1 < units else None
        finish(unit, scores)
        scores = following


def body(
    queries,
    prefix_latent,
    window_latent,
    index_queries,
    index_weights,
    prefix_index_keys,
    window_index_keys,
    picks,
):
    devices = lax.axis_size("ctx")
    own = lax.axis_index("ctx").astype(jnp.int32).reshape(1)
    tok = queries.shape[0]
    per_device = tok // BLK
    span = BLK + tok

    def swap(array, rel):
        return lax.ppermute(array, "ctx", [(i, i ^ rel) for i in range(devices)])

    smem = pl.BlockSpec(memory_space=pltpu.SMEM)
    vmem = pl.BlockSpec(memory_space=pltpu.VMEM)
    params = pltpu.CompilerParams(vmem_limit_bytes=VMEM)

    def index_cost(keys):
        return pl.CostEstimate(
            flops=2 * tok * IH * IDX * keys * 4, bytes_accessed=2**22, transcendentals=0
        )

    order_scratch = [pltpu.VMEM((devices * BLK, IDX), jnp.bfloat16)]

    def index_window(shard_keys):
        count = shard_keys.shape[0] // span
        return pl.pallas_call(
            functools.partial(index_window_kernel, count),
            out_shape=jax.ShapeDtypeStruct((count, tok, LANES), jnp.float32),
            in_specs=[vmem, vmem, vmem],
            out_specs=vmem,
            compiler_params=params,
            cost_estimate=index_cost(count * tok),
        )(index_queries, weights, shard_keys)

    def after(done, *arrays):
        return lax.optimization_barrier((done, *arrays))[1:]

    bits = []
    bit = devices // 2
    while bit >= 4:
        bits.append(bit)
        bit //= 2

    low, high = bits[-1], bits[:-1]
    rows = jnp.concatenate([prefix_latent, window_latent], 0).reshape(3 * BLK, ROW)
    rows = jnp.pad(rows, ((0, 0), (0, WIDE - ROW)))
    shards = {0: rows}
    line, key_line = [0], jnp.concatenate([prefix_index_keys, window_index_keys], 0)
    (key_line,) = lax.optimization_barrier((key_line,))
    (early_queries, early_weights) = after(rows, index_queries, index_weights.T)
    index_queries, weights = pl.pallas_call(
        weights_kernel,
        out_shape=(
            jax.ShapeDtypeStruct(index_queries.shape, index_queries.dtype),
            jax.ShapeDtypeStruct((tok, IH), jnp.float32),
        ),
        in_specs=[pl.BlockSpec(memory_space=pl.ANY)] * 2,
        out_specs=(vmem, vmem),
        scratch_shapes=[pltpu.VMEM((IH, tok), jnp.float32), pltpu.SemaphoreType.DMA((2,))],
        compiler_params=pltpu.CompilerParams(vmem_limit_bytes=COPY_VMEM),
    )(early_queries, early_weights)
    for bit in bits:
        other = swap(key_line, bit)
        if bit != low:
            (other, held, weights) = lax.optimization_barrier((other, rows, weights))
            for hop in [bit] if bit != high[-1] else [bit, 2, low]:
                shards[hop] = swap(held, hop)
        key_line = jnp.concatenate([key_line, other], 0)
        line = line + [rel ^ bit for rel in line]
    key_side = swap(key_line, 2)
    side = [rel ^ 2 for rel in line]
    key_far = swap(jnp.concatenate([key_line, key_side], 0), 1)
    far = [rel ^ 1 for rel in line + side]

    def send(done, *moves):
        sources = sorted({rel for rel, _ in moves})
        held = dict(zip(sources, after(done, *[shards[rel] for rel in sources])))
        for rel, bit in moves:
            shards[rel ^ bit] = swap(held[rel], bit)

    line_done = index_window(key_line)
    send(line_done, (low, 2), (0, 1))
    def settle(array, done, rels):
        got = lax.optimization_barrier((array, done, *[shards[rel] for rel in rels]))
        shards.update(zip(rels, got[2:]))
        return got[0]

    side_done = index_window(key_side)
    side_done = settle(side_done, weights, [1, 2])
    send(side_done, *[(bit, 2) for bit in high], (2, 1))
    rest = []
    for n, bit in enumerate(high):
        for other in bits[n + 1 :]:
            for rel in [r for r in [bit] + rest if not r & (2 * other - 1) and r & -r > other]:
                (held,) = after(side_done, shards[rel])
                shards[rel ^ other] = swap(held, other)
                rest.append(rel ^ other)
    far_done = index_window(key_far)
    send(far_done, *[(rel, 2) for rel in rest], *[(rel, 1) for rel in bits])
    held = settle(index_queries, far_done, rest + [3, low | 2])
    places = [line, side, far]
    tiles = devices * BLK // TILE
    begun = pl.pallas_call(
        functools.partial(index_prefix_kernel, places, 0, tiles // 2),
        out_shape=jax.ShapeDtypeStruct((tok, tiles // 2 * TILE), jnp.float32),
        in_specs=[smem] + [vmem] * 5,
        out_specs=vmem,
        scratch_shapes=order_scratch,
        compiler_params=params,
        cost_estimate=index_cost(tiles // 2 * TILE),
    )(own, held, weights, key_line, key_side, key_far)
    send(begun, *[(bit | 2, 1) for bit in bits], *[(rel, 1) for rel in rest])
    held = settle(index_queries, begun, [rel ^ 1 for rel in bits] + [rel | 2 for rel in high])
    prefix_index, window_index = pl.pallas_call(
        functools.partial(index_last_kernel, places, tiles // 2, tiles - tiles // 2),
        out_shape=(
            jax.ShapeDtypeStruct((tok, devices * BLK), jnp.float32),
            jax.ShapeDtypeStruct((tok, devices * tok), jnp.float32),
        ),
        in_specs=[smem] + [vmem] * 9,
        out_specs=(vmem, vmem),
        scratch_shapes=order_scratch,
        compiler_params=params,
        cost_estimate=index_cost(tiles // 2 * TILE),
    )(
        own,
        held,
        weights,
        key_line,
        key_side,
        key_far,
        line_done,
        side_done,
        far_done,
        begun,
    )
    send(prefix_index, *[(rel | 2, 1) for rel in rest])
    shards = [shards[rel] for rel in range(devices)]

    count = picks.shape[1] * BLK
    attention = pl.pallas_call(
        functools.partial(attention_kernel, devices),
        grid_spec=pltpu.PrefetchScalarGridSpec(
            num_scalar_prefetch=2,
            grid=(per_device, H // 2 // PAIRS),
            in_specs=[pl.BlockSpec((BLK, PAIRS * 2 * ROW), lambda b, h, *_: (b, h))]
            + [vmem] * devices,
            out_specs=pl.BlockSpec((BLK, PAIRS * 2 * LAT), lambda b, h, *_: (b, h)),
            scratch_shapes=[
                pltpu.VMEM((devices + 2, BLK, WIDE), jnp.bfloat16),
                pltpu.VMEM((count, WIDE), jnp.bfloat16),
                pltpu.VMEM((WIDE, count), jnp.bfloat16),
                pltpu.VMEM((WIDE, count), jnp.bfloat16),
                pltpu.SMEM((devices,), jnp.int32),
            ],
        ),
        out_shape=jax.ShapeDtypeStruct((tok, H * LAT), jnp.bfloat16),
        compiler_params=params,
        cost_estimate=pl.CostEstimate(
            flops=2 * tok * H * count * (WIDE + LAT), bytes_accessed=2**24, transcendentals=0
        ),
    )(own, picks, queries, *shards)
    return (attention, prefix_index, window_index)


def solution(mesh):
    placed = P(("groups", "ctx"), None)
    return jax.shard_map(
        body,
        mesh=mesh,
        in_specs=(placed,) * 8,
        out_specs=(placed,) * 3,
        check_vma=False,
    )
```
